32 devices in a mesh: freq: 4 (over x, core), space: 8 (over z, y).
Axes of the slice: x: 2, y: 2, z: 4, core: 2. Of those that a mesh axis runs over, the one named last changes fastest.
Arguments:
- saved_modes: bfloat16 [4, 4, 2, 2, 3, 128, 128, 128], P('freq', None, None, None, None, 'space'), may hold values from -6 to 6
- mode_gains: float32 [4, 4], P('freq'), may hold values from 0.5 to 4
Outputs:
- smoothed_gradient: float32 [128, 128, 128], P('space', 'freq')
The draws below stay inside these ranges and needn't reach their ends.
All inputs are finite; a program needn't handle non-finite values.
Results may differ from the reference program's by a relative error of at most 0.0003.
Values may be sent and summed in bfloat16 or wider, within the bound.
No kernel may reach another device: no remote copies, remote signals or barrier semaphores. Data moves between devices by JAX's collectives and lax.ppermute only.
A program may use at most 256 MiB of HBM per device.

```python
import math
import jax
import jax.numpy as jnp
from jax import lax

NY = 128
NZ = 128
MODES = 4
NX = 128
FREQS = 4


def block_scale(own_key, dims, pieces, least, largest):
    level, own = 1.0, jax.random.fold_in(own_key, 6)
    for position, shards_of in pieces:
        heights = jnp.exp(jax.random.uniform(jax.random.fold_in(own, position), (shards_of,), jnp.float32, least / len(pieces), largest / len(pieces)))
        level = level * jnp.repeat(heights, dims[position] // shards_of).reshape([-1 if axis == position else 1 for axis in range(len(dims))])
    return level


def scatter_about(own_key, extent, spread, reach, split=(), kind=jnp.bfloat16):
    entries = jax.random.normal(own_key, extent, jnp.float32) * spread
    if len(split) > 0:
        entries = block_scale(own_key, extent, split, -0.22, 0.18) * entries
    return jnp.clip(entries, min=-reach, max=reach).astype(kind)


def setup_inputs(seed: int = 0) -> dict:
    key_list = jax.random.split(jax.random.key(seed), 3)
    return {
        "saved_modes": scatter_about(key_list[0], (FREQS, MODES, 2, 2, 3, NX, NY, NZ), 1.0, 6.0, ((0, 4), (5, 8))),
        "mode_gains": jnp.clip(jnp.exp(math.log(4.0) - 2.0794415 * jax.random.uniform(key_list[1], (FREQS, MODES), jnp.float32) ** block_scale(key_list[1], (FREQS, MODES), ((0, 4),), -0.2, 0.2)), 0.5, 4.0),
    }


AXIAL = 0.35
CROSS = 0.06


def central_diffs(grid_values):
    padded = jnp.pad(grid_values, ((0, 0), (0, 0), (1, 1), (1, 1), (1, 1)))
    along_x = (padded[:, :, 2:, 1:-1, 1:-1] - padded[:, :, :-2, 1:-1, 1:-1]) * 0.5
    along_y = (padded[:, :, 1:-1, 2:, 1:-1] - padded[:, :, 1:-1, :-2, 1:-1]) * 0.5
    along_z = (padded[:, :, 1:-1, 1:-1, 2:] - padded[:, :, 1:-1, 1:-1, :-2]) * 0.5
    return (along_x, along_y, along_z)


def strain_dot(grad_forward, grad_adjoint):
    running = jnp.zeros(grad_forward[0].shape[2:], jnp.float32)
    for row_axis in range(3):
        for col_axis in range(3):
            strain_u = 0.5 * (grad_forward[row_axis][:, col_axis] + grad_forward[col_axis][:, row_axis])
            strain_v = 0.5 * (grad_adjoint[row_axis][:, col_axis] + grad_adjoint[col_axis][:, row_axis])
            running = running + jnp.sum(strain_u * strain_v, axis=0)
    return running


def smooth_pass(grid_values):
    padded = jnp.pad(grid_values, 1)
    center = grid_values
    axial = padded[2:, 1:-1, 1:-1] + padded[:-2, 1:-1, 1:-1] - 2.0 * center
    cross = padded[1:-1, 2:, 1:-1] + padded[1:-1, :-2, 1:-1] + padded[1:-1, 1:-1, 2:] + padded[1:-1, 1:-1, :-2] - 4.0 * center
    return center + AXIAL * axial + CROSS * cross


def reference(saved_modes, mode_gains):
    freq_total = saved_modes.shape[0]
    mode_count = saved_modes.shape[1]
    factor = -2.0 / (freq_total * mode_count)

    def one_pair(pair_index, running):
        freq_index = pair_index // mode_count
        mode_index = pair_index % mode_count
        mode_pair = lax.dynamic_index_in_dim(saved_modes, freq_index, 0, False)
        mode_pair = lax.dynamic_index_in_dim(mode_pair, mode_index, 0, False).astype(jnp.float32)
        weight = lax.dynamic_index_in_dim(lax.dynamic_index_in_dim(mode_gains, freq_index, 0, False), mode_index, 0, False)
        return running + (factor * weight) * strain_dot(central_diffs(mode_pair[0]), central_diffs(mode_pair[1]))

    sensitivity = lax.fori_loop(0, freq_total * mode_count, one_pair, jnp.zeros(saved_modes.shape[5:], jnp.float32))
    for sweep in range(3):
        sensitivity = smooth_pass(sensitivity)
    return sensitivity
```

```python
import functools

import jax
import jax.numpy as jnp
from jax import lax
from jax.experimental import pallas as pl
from jax.experimental.pallas import tpu as pltpu
from jax.sharding import PartitionSpec as P

AXIAL = 0.35
CROSS = 0.06
MARGIN = 8
VMEM_LIMIT = 48 * 1024 * 1024


def strain_terms(field, row_grad, lane_grad, axial_grad):
    normal = (
        axial_grad(0),
        axial_grad(1) + row_grad(0),
        axial_grad(2) + lane_grad(0),
    )
    inner = (row_grad(1), lane_grad(2), row_grad(2) + lane_grad(1))
    return normal, inner


def interior_kernel(side_ref, weight_ref, modes_ref, sens_ref, edge_ref, wide_ref, lane_ref):
    slab, rows, lanes = modes_ref.shape[2:]
    first = (pl.program_id(0) == 0) & (pl.program_id(1) == 0)

    @pl.when(first)
    def _():
        sens_ref[...] = jnp.zeros_like(sens_ref)
        wide_ref[...] = jnp.zeros_like(wide_ref)

    source = lax.broadcasted_iota(jnp.int32, (lanes, lanes), 0)
    target = lax.broadcasted_iota(jnp.int32, (lanes, lanes), 1)
    difference = jnp.where(source == target + 1, 1.0, 0.0) - jnp.where(source == target - 1, 1.0, 0.0)
    difference = difference.astype(jnp.bfloat16)
    scale = weight_ref[0, pl.program_id(0)]

    def load_plane(plane, carry):
        for kind in range(2):
            for part in range(3):
                values = modes_ref[kind, part, plane]
                field = kind * 3 + part
                wide_ref[field, plane + 1, MARGIN : MARGIN + rows] = values.astype(jnp.float32)
                lane_ref[field, plane] = jnp.dot(
                    values, difference, preferred_element_type=jnp.float32
                )
        return carry

    lax.fori_loop(0, slab, load_plane, 0)

    step = 16

    def terms(plane, start):
        sides = []
        for kind in range(2):
            def axial(part):
                field = kind * 3 + part
                return (
                    wide_ref[field, plane + 2, pl.ds(MARGIN + start, step)]
                    - wide_ref[field, plane, pl.ds(MARGIN + start, step)]
                )

            def by_row(part):
                field = kind * 3 + part
                return (
                    wide_ref[field, plane + 1, pl.ds(MARGIN + start + 1, step)]
                    - wide_ref[field, plane + 1, pl.ds(MARGIN + start - 1, step)]
                )

            def by_lane(part):
                return lane_ref[kind * 3 + part, plane, pl.ds(start, step)]

            sides.append(strain_terms(None, by_row, by_lane, axial))
        return sides

    def inner_plane(plane, carry):
        for start in range(0, rows, step):
            (nu, iu), (nv, iv) = terms(plane, start)
            diagonal = nu[0] * nv[0] + iu[0] * iv[0] + iu[1] * iv[1]
            mixed = nu[1] * nv[1] + nu[2] * nv[2] + iu[2] * iv[2]
            sens_ref[plane, pl.ds(MARGIN + start, step)] += scale * (2.0 * diagonal + mixed)
        return carry

    lax.fori_loop(1, slab - 1, inner_plane, 0)

    for plane, sign in ((0, -1.0), (slab - 1, 1.0)):
        side = 1 - side_ref[0] if plane == 0 else side_ref[0]
        for start in range(0, rows, step):
            (nu, iu), (nv, iv) = terms(plane, start)
            diagonal = iu[0] * iv[0] + iu[1] * iv[1]
            mixed = iu[2] * iv[2]
            sens_ref[plane, pl.ds(MARGIN + start, step)] += scale * (2.0 * diagonal + mixed)
            for part in range(3):
                edge_ref[side, 0, part, pl.ds(start, step)] = sign * nu[part]
                edge_ref[side, 1, part, pl.ds(start, step)] = sign * nv[part]


def interior(saved_modes, weights, odd):
    _, modes, kinds, halves, parts, slab, rows, lanes = saved_modes.shape
    return pl.pallas_call(
        interior_kernel,
        grid=(modes, halves),
        in_specs=[
            pl.BlockSpec(memory_space=pltpu.SMEM),
            pl.BlockSpec(memory_space=pltpu.SMEM),
            pl.BlockSpec(
                (None, None, kinds, None, parts, slab, rows, lanes),
                lambda m, c: (0, m, 0, c, 0, 0, 0, 0),
            ),
        ],
        out_specs=[
            pl.BlockSpec((slab, rows + 2 * MARGIN, lanes), lambda m, c: (0, 0, 0)),
            pl.BlockSpec(
                (2, None, None, kinds, parts, rows, lanes),
                lambda m, c: (0, m, c, 0, 0, 0, 0),
            ),
        ],
        out_shape=[
            jax.ShapeDtypeStruct((slab, rows + 2 * MARGIN, lanes), jnp.float32),
            jax.ShapeDtypeStruct((2, modes, halves, kinds, parts, rows, lanes), jnp.float32),
        ],
        scratch_shapes=[
            pltpu.VMEM((kinds * parts, slab + 2, rows + 2 * MARGIN, lanes), jnp.float32),
            pltpu.VMEM((kinds * parts, slab, rows, lanes), jnp.float32),
        ],
        compiler_params=pltpu.CompilerParams(vmem_limit_bytes=VMEM_LIMIT),
        cost_estimate=pl.CostEstimate(
            flops=saved_modes.size * 16, bytes_accessed=saved_modes.size * 2, transcendentals=0
        ),
    )(odd, weights, saved_modes)


def late_kernel(weight_ref, edge_ref, halo_ref, out_ref):
    mode = pl.program_id(0)
    halves = edge_ref.shape[0]
    total = None
    for half in range(halves):
        diagonal, mixed = None, None
        for part in range(3):
            u = edge_ref[half, 0, part] + halo_ref[0, half, part].astype(jnp.float32)
            v = edge_ref[half, 1, part] + halo_ref[1, half, part].astype(jnp.float32)
            term = u * v
            if part == 0:
                term = 2.0 * term
            total = term if total is None else total + term
    total = weight_ref[0, mode] * total

    @pl.when(mode == 0)
    def _():
        out_ref[...] = jnp.zeros_like(out_ref)

    rows = total.shape[0]
    out_ref[pl.ds(MARGIN, rows)] += total


def late(weights, edges, halo, side):
    _, modes, halves, kinds, parts, rows, lanes = edges.shape
    return pl.pallas_call(
        late_kernel,
        grid=(modes,),
        in_specs=[
            pl.BlockSpec(memory_space=pltpu.SMEM),
            pl.BlockSpec(
                (None, None, halves, kinds, parts, rows, lanes),
                lambda m: (side, m, 0, 0, 0, 0, 0),
            ),
            pl.BlockSpec(
                (None, kinds, halves, parts, rows, lanes), lambda m: (m, 0, 0, 0, 0, 0)
            ),
        ],
        out_specs=pl.BlockSpec((rows + 2 * MARGIN, lanes), lambda m: (0, 0)),
        out_shape=jax.ShapeDtypeStruct((rows + 2 * MARGIN, lanes), jnp.float32),
        compiler_params=pltpu.CompilerParams(vmem_limit_bytes=VMEM_LIMIT),
    )(weights, edges, halo)


def smooth_kernel(total_x, total_y, place_ref, base_ref, *refs):
    near_ref, far_ref = refs[:2]
    late_refs = refs[2:-3]
    out_ref, one_ref, two_ref = refs[-3:]
    slab, tall, lanes = base_ref.shape
    odd, first_x, first_y = place_ref[0], place_ref[1], place_ref[2]
    even = odd == 0
    one_ref[pl.ds(3, slab)] = base_ref[...]
    near = near_ref[...]
    far = far_ref[...]
    one_ref[pl.ds(0, 3)] = jnp.where(even, far, near)
    one_ref[pl.ds(slab + 3, 3)] = jnp.where(even, near, far)
    late = late_refs[0][...]
    for ref in late_refs[1:]:
        late = late + ref[...]
    low, high = 3, slab + 2
    one_ref[high] += jnp.where(even, late[0], late[1])
    one_ref[low] += jnp.where(even, late[1], late[0])
    one_ref[high + 1] += jnp.where(even, late[2], late[3])
    one_ref[low - 1] += jnp.where(even, late[3], late[2])

    lane = lax.broadcasted_iota(jnp.int32, (tall, lanes), 1)
    row = lax.broadcasted_iota(jnp.int32, (tall, lanes), 0) + (first_y - MARGIN)
    first_lane, last_lane = lane == 0, lane == lanes - 1
    inside_y = (row >= 0) & (row < total_y)

    def passed(source, plane):
        center = source[plane]
        axial = source[plane + 1] + source[plane - 1] - 2.0 * center
        cross = (
            pltpu.roll(center, tall - 1, 0)
            + pltpu.roll(center, 1, 0)
            + jnp.where(last_lane, 0.0, pltpu.roll(center, lanes - 1, 1))
            + jnp.where(first_lane, 0.0, pltpu.roll(center, 1, 1))
            - 4.0 * center
        )
        x = first_x + (plane - 3)
        inside = inside_y & (x >= 0) & (x < total_x)
        return jnp.where(inside, center + AXIAL * axial + CROSS * cross, 0.0)

    for plane in range(1, slab + 5):
        two_ref[plane] = passed(one_ref, plane)
    for plane in range(2, slab + 4):
        one_ref[plane] = passed(two_ref, plane)
    for plane in range(3, slab + 3):
        out_ref[plane - 3] = passed(one_ref, plane)[MARGIN : tall - MARGIN]


def smooth(place, base, near, far, lates, total_x, total_y):
    slab, tall, lanes = base.shape
    return pl.pallas_call(
        functools.partial(smooth_kernel, total_x, total_y),
        in_specs=[pl.BlockSpec(memory_space=pltpu.SMEM)]
        + [pl.BlockSpec(memory_space=pltpu.VMEM)] * (3 + len(lates)),
        out_specs=pl.BlockSpec(memory_space=pltpu.VMEM),
        out_shape=jax.ShapeDtypeStruct((slab, tall - 2 * MARGIN, lanes), jnp.float32),
        scratch_shapes=[pltpu.VMEM((slab + 6, tall, lanes), jnp.float32)] * 2,
        compiler_params=pltpu.CompilerParams(vmem_limit_bytes=VMEM_LIMIT),
    )(place, base, near, far, *lates)


def swap(block, axis, pairs):
    return lax.ppermute(block, axis, [p for a, b in pairs for p in ((a, b), (b, a))])


def band(block, index, band_rows):
    start = pl.multiple_of(index * band_rows, 8)
    return lax.dynamic_slice_in_dim(block, start, band_rows + 2 * MARGIN, axis=1)


def shares(block, band_rows):
    count = lax.axis_size("freq")
    mine = lax.axis_index("freq")
    found = [band(block, mine, band_rows)]
    for turn in range(1, count):
        part = band(block, (mine + turn) % count, band_rows)
        found.append(lax.ppermute(part, "freq", [(i, (i + turn) % count) for i in range(count)]))
    return found


def local(saved_modes, mode_gains):
    _, modes, kinds, halves, parts, slab, rows, lanes = saved_modes.shape
    freqs = lax.axis_size("freq")
    slabs = lax.axis_size("space")
    factor = -2.0 / (saved_modes.shape[0] * freqs * modes)
    weights = (factor / 8.0) * mode_gains
    place = lax.axis_index("space")
    odd = place % 2
    band_rows = rows // freqs
    near_pairs = [(i, i + 1) for i in range(0, slabs - 1, 2)]
    far_pairs = [(i, i + 1) for i in range(1, slabs - 1, 2)]

    near_plane = jnp.where(odd == 0, slab - 1, 0)
    far_plane = slab - 1 - near_plane
    near_halo = swap(lax.dynamic_index_in_dim(saved_modes[0], near_plane, 4, False), "space", near_pairs)
    far_halo = swap(lax.dynamic_index_in_dim(saved_modes[0], far_plane, 4, False), "space", far_pairs)

    early, edges = interior(saved_modes, weights, odd.reshape(1).astype(jnp.int32))
    base = functools.reduce(jnp.add, shares(early, band_rows))
    near_start = jnp.where(odd == 0, slab - 3, 0)
    near = swap(lax.dynamic_slice_in_dim(base, near_start, 3, 0), "space", near_pairs)
    far = swap(lax.dynamic_slice_in_dim(base, slab - 3 - near_start, 3, 0), "space", far_pairs)

    near_late = late(weights, edges, near_halo, 0)
    far_late = late(weights, edges, far_halo, 1)
    others = [swap(near_late, "space", near_pairs), swap(far_late, "space", far_pairs)]
    lates = shares(jnp.stack([near_late, far_late] + others), band_rows)
    where = jnp.stack([odd, place * slab, lax.axis_index("freq") * band_rows]).astype(jnp.int32)
    return smooth(where, base, near, far, lates, slab * slabs, rows)


def solution(mesh):
    in_specs = (P("freq", None, None, None, None, "space", None, None), P("freq", None))
    out_specs = P("space", "freq", None)
    return jax.shard_map(local, mesh=mesh, in_specs=in_specs, out_specs=out_specs, check_vma=False)
```

```python
import functools

import jax
import jax.numpy as jnp
from jax import lax
from jax.experimental import pallas as pl
from jax.experimental.pallas import tpu as pltpu
from jax.sharding import PartitionSpec as P

AXIAL = 0.35
CROSS = 0.06
MARGIN = 8
STEP = 16
INTERIOR_VMEM = 36 * 1024 * 1024
QUICK = pl.CostEstimate(flops=1024, bytes_accessed=1024, transcendentals=0)
INTERIOR_FLOPS = 8 * 10**9
SMOOTH_FLOPS = 10**10
SMALL_VMEM = 16 * 1024 * 1024


def plane_kernel(begin, plane_ref, modes_ref, *refs):
    out_refs, sems = refs[-1 - len(begin) : -1], refs[-1]
    copies = []
    for at, (first, out_ref) in enumerate(zip(begin, out_refs, strict=True)):
        source = modes_ref.at[0, pl.ds(first, out_ref.shape[0]), :, :, :, plane_ref[0]]
        copies.append(pltpu.make_async_copy(source, out_ref, sems.at[at]))
        copies[-1].start()
    for copy in copies:
        copy.wait()


def planes(saved_modes, plane, groups, after):
    _, _, kinds, halves, parts, _, rows, lanes = saved_modes.shape
    return pl.pallas_call(
        functools.partial(plane_kernel, [first for first, _ in groups]),
        in_specs=[pl.BlockSpec(memory_space=pltpu.SMEM), pl.BlockSpec(memory_space=pl.ANY)]
        + [pl.BlockSpec(memory_space=pl.ANY)] * len(after),
        out_specs=[pl.BlockSpec(memory_space=pltpu.VMEM)] * len(groups),
        out_shape=[
            pltpu.VMEM((count, kinds, halves, parts, rows, lanes), saved_modes.dtype) for _, count in groups
        ],
        scratch_shapes=[pltpu.SemaphoreType.DMA((len(groups),))],
        compiler_params=pltpu.CompilerParams(vmem_limit_bytes=SMALL_VMEM),
        cost_estimate=QUICK,
    )(plane.reshape(1).astype(jnp.int32), hbm(saved_modes), *after)


def interior_kernel(after, side_ref, weight_ref, modes_ref, *refs):
    sens_ref, near_edge_ref, far_edge_ref, wide_ref, lane_ref = refs[after:]
    slab, rows, lanes = modes_ref.shape[2:]

    @pl.when((pl.program_id(0) == 0) & (pl.program_id(1) == 0))
    def _():
        sens_ref[...] = jnp.zeros_like(sens_ref)
        wide_ref[...] = jnp.zeros_like(wide_ref)

    source = lax.broadcasted_iota(jnp.int32, (lanes, lanes), 0)
    target = lax.broadcasted_iota(jnp.int32, (lanes, lanes), 1)
    difference = jnp.where(source == target + 1, 1.0, 0.0) - jnp.where(source == target - 1, 1.0, 0.0)
    difference = difference.astype(jnp.bfloat16)
    lane = lax.broadcasted_iota(jnp.int32, (STEP, lanes), 1)
    not_last = jnp.where(lane == lanes - 1, 0.0, 1.0)
    not_first = jnp.where(lane == 0, 0.0, 1.0)
    scale = weight_ref[0, pl.program_id(0)]

    def load_plane(plane):
        for kind in range(2):
            for part in range(3):
                values = modes_ref[kind, part, plane]
                field = kind * 3 + part
                wide_ref[field, plane + 1, MARGIN : MARGIN + rows] = values.astype(jnp.float32)
                if part > 0:
                    lane_ref[field, plane] = jnp.dot(
                        values, difference, preferred_element_type=jnp.float32
                    )

    def terms(plane, start):
        sides = []
        for kind in range(2):

            def axial(part):
                field = kind * 3 + part
                return (
                    wide_ref[field, plane + 2, pl.ds(MARGIN + start, STEP)]
                    - wide_ref[field, plane, pl.ds(MARGIN + start, STEP)]
                )

            def by_row(part):
                field = kind * 3 + part
                return (
                    wide_ref[field, plane + 1, pl.ds(MARGIN + start + 1, STEP)]
                    - wide_ref[field, plane + 1, pl.ds(MARGIN + start - 1, STEP)]
                )

            def by_lane(part):
                if part > 0:
                    return lane_ref[kind * 3 + part, plane, pl.ds(start, STEP)]
                values = modes_ref[kind, part, plane, pl.ds(start, STEP)]
                upper = pltpu.roll(values, lanes - 1, 1).astype(jnp.float32)
                lower = pltpu.roll(values, 1, 1).astype(jnp.float32)
                return upper * not_last - lower * not_first

            outer = (axial(0), axial(1) + by_row(0), axial(2) + by_lane(0))
            inner = (by_row(1), by_lane(2), by_row(2) + by_lane(1))
            sides.append((outer, inner))
        return sides

    def inner_plane(plane):
        for start in range(0, rows, STEP):
            (ou, iu), (ov, iv) = terms(plane, start)
            diagonal = ou[0] * ov[0] + iu[0] * iv[0] + iu[1] * iv[1]
            mixed = ou[1] * ov[1] + ou[2] * ov[2] + iu[2] * iv[2]
            sens_ref[plane, pl.ds(MARGIN + start, STEP)] += scale * (2.0 * diagonal + mixed)

    def both(plane, carry):
        load_plane(plane + 1)
        inner_plane(plane)
        return carry

    load_plane(0)
    load_plane(1)
    lax.fori_loop(1, slab - 1, both, 0, unroll=True)

    odd = side_ref[0]
    near = (1 - odd) * (slab - 1)
    for edge_ref, plane, sign in (
        (near_edge_ref, near, 1.0 - 2.0 * odd.astype(jnp.float32)),
        (far_edge_ref, slab - 1 - near, 2.0 * odd.astype(jnp.float32) - 1.0),
    ):
        for start in range(0, rows, STEP):
            (ou, iu), (ov, iv) = terms(plane, start)
            diagonal = iu[0] * iv[0] + iu[1] * iv[1]
            mixed = iu[2] * iv[2]
            sens_ref[plane, pl.ds(MARGIN + start, STEP)] += scale * (2.0 * diagonal + mixed)
            for part in range(3):
                edge_ref[0, part, pl.ds(start, STEP)] = sign * ou[part]
                edge_ref[1, part, pl.ds(start, STEP)] = sign * ov[part]


def interior(saved_modes, weights, sides, after):
    _, modes, kinds, halves, parts, slab, rows, lanes = saved_modes.shape
    whole = (slab, rows + 2 * MARGIN, lanes)
    edges = (modes, halves, kinds, parts, rows, lanes)
    fields = kinds * parts
    return pl.pallas_call(
        functools.partial(interior_kernel, len(after)),
        grid=(modes, halves),
        in_specs=[
            pl.BlockSpec(memory_space=pltpu.SMEM),
            pl.BlockSpec(memory_space=pltpu.SMEM),
            pl.BlockSpec(
                (None, None, kinds, None, parts, slab, rows, lanes),
                lambda m, c: (0, m, 0, c, 0, 0, 0, 0),
            ),
        ]
        + [pl.BlockSpec(memory_space=pl.ANY)] * len(after),
        out_specs=[pl.BlockSpec(whole, lambda m, c: (0, 0, 0))]
        + [pl.BlockSpec((None, None) + edges[2:], lambda m, c: (m, c, 0, 0, 0, 0))] * 2,
        out_shape=[pltpu.VMEM(whole, jnp.float32), pltpu.HBM(edges, jnp.float32), pltpu.VMEM(edges, jnp.float32)],
        scratch_shapes=[
            pltpu.VMEM((fields, slab + 2, rows + 2 * MARGIN, lanes), jnp.float32),
            pltpu.VMEM((fields, slab, rows, lanes), jnp.float32),
        ],
        compiler_params=pltpu.CompilerParams(vmem_limit_bytes=INTERIOR_VMEM),
        cost_estimate=pl.CostEstimate(flops=INTERIOR_FLOPS, bytes_accessed=1024, transcendentals=0),
    )(sides, weights, saved_modes, *after)


def outer_plane(weight_ref, edge_ref, halo_ref, begin, start):
    modes, halves, _, parts = edge_ref.shape[:4]
    total = None
    for mode in range(modes):
        found = None
        for half in range(halves):
            for part in range(parts):
                u, v = (
                    edge_ref[mode, half, kind, part, pl.ds(start, STEP)]
                    + halo_ref[mode, kind, half, part, pl.ds(start, STEP)].astype(jnp.float32)
                    for kind in range(2)
                )
                term = u * v
                if part == 0:
                    term = 2.0 * term
                found = term if found is None else found + term
        found = weight_ref[0, begin + mode] * found
        total = found if total is None else total + found
    return total


def far_kernel(side_ref, weight_ref, edge_ref, halo_ref, sens_ref, turns_ref, tall_ref):
    slab = sens_ref.shape[0]
    rows = edge_ref.shape[4]
    count, _, tall, _ = turns_ref.shape
    band = tall - 2 * MARGIN
    far = side_ref[0] * (slab - 1)
    tall_ref[...] = sens_ref[far]
    for start in range(0, rows, STEP):
        tall_ref[pl.ds(MARGIN + start, STEP)] += outer_plane(weight_ref, edge_ref, halo_ref, 0, start)
    for piece in range(count):
        index, bits = 0, 1
        while bits < count:
            index = 2 * index + (piece // bits) % 2
            bits *= 2
        turns_ref[piece] = sens_ref[:, pl.ds(index * band, tall)]
        turns_ref[piece, far] = tall_ref[pl.ds(index * band, tall)]


def finish_far(sides, weights, edges, halo, sens, freqs):
    slab, rows, lanes = sens.shape
    band = (rows - 2 * MARGIN) // freqs
    return pl.pallas_call(
        far_kernel,
        in_specs=[pl.BlockSpec(memory_space=pltpu.SMEM)] * 2 + [pl.BlockSpec(memory_space=pltpu.VMEM)] * 3,
        out_specs=pl.BlockSpec(memory_space=pltpu.VMEM),
        out_shape=jax.ShapeDtypeStruct((freqs, slab, band + 2 * MARGIN, lanes), jnp.float32),
        scratch_shapes=[pltpu.VMEM((rows, lanes), jnp.float32)],
        compiler_params=pltpu.CompilerParams(vmem_limit_bytes=SMALL_VMEM),
        cost_estimate=QUICK,
    )(sides, weights, edges, halo, sens)


def near_part_kernel(weight_ref, edge_ref, halo_ref, last_ref, *refs):
    out_ref, kept_ref, done = refs[-3:]
    copy = pltpu.make_async_copy(last_ref.at[last_ref.shape[0] - 1], kept_ref.at[0], done)
    copy.start()
    for start in range(0, out_ref.shape[0], STEP):
        out_ref[pl.ds(start, STEP)] = outer_plane(weight_ref, edge_ref, halo_ref, 0, start)
    copy.wait()


def near_part(weights, edges, halo, after):
    count = halo.shape[0]
    rows, lanes = edges.shape[4:]
    return pl.pallas_call(
        near_part_kernel,
        grid=(1,),
        in_specs=[
            pl.BlockSpec(memory_space=pltpu.SMEM),
            pl.BlockSpec((count,) + edges.shape[1:], lambda i: (0,) * 6),
            pl.BlockSpec(halo.shape, lambda i: (0,) * 6),
        ]
        + [pl.BlockSpec(memory_space=pl.ANY)] * (1 + len(after)),
        out_specs=[
            pl.BlockSpec((rows, lanes), lambda i: (0, 0)),
            pl.BlockSpec(memory_space=pltpu.VMEM),
        ],
        out_shape=[
            pltpu.VMEM((rows, lanes), jnp.float32),
            pltpu.VMEM((1,) + edges.shape[1:], jnp.float32),
        ],
        scratch_shapes=[pltpu.SemaphoreType.DMA(())],
        compiler_params=pltpu.CompilerParams(vmem_limit_bytes=SMALL_VMEM),
        cost_estimate=QUICK,
    )(weights, edges, halo, edges, *after)


def outer_kernel(begin, weight_ref, edge_ref, halo_ref, before_ref, *refs):
    out_ref, tall_ref, band_ref, done = refs[-4:]
    rows = edge_ref.shape[4]
    pieces, tall, lanes = band_ref.shape
    band = tall - 2 * MARGIN
    empty = jnp.zeros((MARGIN, lanes), jnp.float32)
    tall_ref[pl.ds(0, MARGIN)] = empty
    tall_ref[pl.ds(MARGIN + rows, MARGIN)] = empty
    for start in range(0, rows, STEP):
        found = outer_plane(weight_ref, edge_ref, halo_ref, begin, start)
        tall_ref[pl.ds(MARGIN + start, STEP)] = before_ref[pl.ds(start, STEP)] + found
    for piece in range(pieces):
        band_ref[piece] = tall_ref[pl.ds(piece // 2 * band, tall)]
    copy = pltpu.make_async_copy(band_ref, out_ref, done)
    copy.start()
    copy.wait()


def finish_near(begin, weights, edges, halo, before, pieces, after):
    rows, lanes = edges.shape[4:]
    shape = (pieces, rows // (pieces // 2) + 2 * MARGIN, lanes)
    return pl.pallas_call(
        functools.partial(outer_kernel, begin),
        in_specs=[pl.BlockSpec(memory_space=pltpu.SMEM)]
        + [pl.BlockSpec(memory_space=pltpu.VMEM)] * 3
        + [pl.BlockSpec(memory_space=pl.ANY)] * len(after),
        out_specs=pl.BlockSpec(memory_space=pltpu.HBM),
        out_shape=pltpu.HBM(shape, jnp.float32),
        scratch_shapes=[
            pltpu.VMEM((rows + 2 * MARGIN, lanes), jnp.float32),
            pltpu.VMEM(shape, jnp.float32),
            pltpu.SemaphoreType.DMA(()),
        ],
        compiler_params=pltpu.CompilerParams(vmem_limit_bytes=SMALL_VMEM),
        cost_estimate=QUICK,
    )(weights, edges, halo, before, *after)


class Pass:
    def __init__(self, tall, lanes, first_y, total_y):
        self.tall, self.lanes = tall, lanes
        self.lane = lax.broadcasted_iota(jnp.int32, (tall, lanes), 1)
        row = lax.broadcasted_iota(jnp.int32, (tall, lanes), 0) + (first_y - MARGIN)
        self.inside = (row >= 0) & (row < total_y)

    def __call__(self, below, center, above):
        axial = above + below - 2.0 * center
        cross = (
            pltpu.roll(center, self.tall - 1, 0)
            + pltpu.roll(center, 1, 0)
            + jnp.where(self.lane == self.lanes - 1, 0.0, pltpu.roll(center, self.lanes - 1, 1))
            + jnp.where(self.lane == 0, 0.0, pltpu.roll(center, 1, 1))
            - 4.0 * center
        )
        return jnp.where(self.inside, center + AXIAL * axial + CROSS * cross, 0.0)


def smooth_kernel(total_x, total_y, place_ref, base_ref, near_ref, far_ref, out_ref, one_ref, two_ref):
    slab, tall, lanes = base_ref.shape
    first_x = place_ref[1]
    even = place_ref[0] == 0
    one_ref[pl.ds(3, slab)] = base_ref[...]
    near = near_ref[...]
    far = far_ref[...]
    one_ref[pl.ds(0, 3)] = jnp.where(even, far, near)
    one_ref[pl.ds(slab + 3, 3)] = jnp.where(even, near, far)
    smoothed = Pass(tall, lanes, place_ref[2], total_y)

    def clear(ref, plane):
        x = first_x + (plane - 3)

        @pl.when((x < 0) | (x >= total_x))
        def _():
            ref[plane] = jnp.zeros_like(ref[plane])

    def passed(source, plane):
        return smoothed(source[plane - 1], source[plane], source[plane + 1])

    for plane in range(1, slab + 5):
        two_ref[plane] = passed(one_ref, plane)
    for plane in (1, 2, slab + 3, slab + 4):
        clear(two_ref, plane)
    for plane in range(2, slab + 4):
        one_ref[plane] = passed(two_ref, plane)
    for plane in (2, slab + 3):
        clear(one_ref, plane)
    for plane in range(3, slab + 3):
        out_ref[plane - 3] = passed(one_ref, plane)[MARGIN : tall - MARGIN]


def smooth(place, base, near, far, total_x, total_y):
    slab, tall, lanes = base.shape
    return pl.pallas_call(
        functools.partial(smooth_kernel, total_x, total_y),
        in_specs=[pl.BlockSpec(memory_space=pltpu.SMEM)]
        + [pl.BlockSpec(memory_space=pltpu.VMEM)] * 3,
        out_specs=pl.BlockSpec(memory_space=pltpu.VMEM),
        out_shape=pltpu.VMEM((slab, tall - 2 * MARGIN, lanes), jnp.float32),
        scratch_shapes=[pltpu.VMEM((slab + 6, tall, lanes), jnp.float32)] * 2,
        compiler_params=pltpu.CompilerParams(vmem_limit_bytes=SMALL_VMEM),
        cost_estimate=pl.CostEstimate(flops=SMOOTH_FLOPS, bytes_accessed=1024, transcendentals=0),
    )(place, base, near, far)


def add_near_kernel(total_y, place_ref, late_vmem, before_ref, out_ref):
    pieces, tall, lanes = late_vmem.shape
    slab, band = before_ref.shape[:2]
    even = place_ref[0] == 0
    first = jnp.where(even, slab - 4, 0)
    out_ref[...] = before_ref[...]
    smoothed = Pass(tall, lanes, place_ref[2], total_y)
    lower, upper = (
        functools.reduce(jnp.add, [late_vmem[i] for i in range(which, pieces, 2)]) for which in range(2)
    )
    zero = jnp.zeros_like(lower)
    planes = {-1: jnp.where(even, upper, lower), 0: jnp.where(even, lower, upper)}
    for reach in (1, 2, 3):
        low, high = max(-1 - reach, reach - 4), min(reach, 3)
        planes = {
            at: smoothed(planes.get(at - 1, zero), planes.get(at, zero), planes.get(at + 1, zero))
            for at in range(low, high + 1)
        }
    for at in range(4):
        out_ref[first + jnp.where(even, 3 - at, at)] += planes[at][MARGIN : tall - MARGIN]


def add_near(place, late, before, total_y):
    slab, band, lanes = before.shape
    return pl.pallas_call(
        functools.partial(add_near_kernel, total_y),
        in_specs=[pl.BlockSpec(memory_space=pltpu.SMEM)] + [pl.BlockSpec(memory_space=pltpu.VMEM)] * 2,
        out_specs=pl.BlockSpec(memory_space=pltpu.VMEM),
        out_shape=jax.ShapeDtypeStruct(before.shape, jnp.float32),
        compiler_params=pltpu.CompilerParams(vmem_limit_bytes=SMALL_VMEM),
        cost_estimate=QUICK,
    )(place, late, before)


def swap(block, axis, pairs):
    return lax.ppermute(block, axis, [p for a, b in pairs for p in ((a, b), (b, a))])


def trade(pieces, pairs):
    slabs = lax.axis_size("space")
    groups = [[f * slabs + s for f in range(lax.axis_size("freq")) for s in pair] for pair in pairs]
    return lax.all_to_all(pieces, ("freq", "space"), 0, 0, axis_index_groups=groups, tiled=True)


def hbm(block):
    return pltpu.with_memory_space_constraint(block, pltpu.HBM)


def split_kernel(side_ref, found_ref, send_ref, keep_ref):
    half = keep_ref.shape[0]
    which = side_ref[1] // 2 % 2
    for ref, side in ((keep_ref, which), (send_ref, 1 - which)):
        for piece in range(half):
            at = side * half + piece
            ref[piece] = found_ref[at] + found_ref[2 * half + at]


def split(sides, found):
    shape = (found.shape[0] // 4,) + found.shape[1:]
    return pl.pallas_call(
        split_kernel,
        in_specs=[pl.BlockSpec(memory_space=pltpu.SMEM), pl.BlockSpec(memory_space=pltpu.VMEM)],
        out_specs=[pl.BlockSpec(memory_space=pltpu.VMEM)] * 2,
        out_shape=[jax.ShapeDtypeStruct(shape, jnp.float32)] * 2,
        compiler_params=pltpu.CompilerParams(vmem_limit_bytes=SMALL_VMEM),
        cost_estimate=QUICK,
    )(sides, found)


def base_kernel(side_ref, keep_ref, found_ref, *refs):
    base_ref, near_ref, far_ref = refs[-3:]
    slab, depth = base_ref.shape[0], near_ref.shape[0]
    base_ref[...] = keep_ref[0] + found_ref[0]
    start = (1 - side_ref[0]) * (slab - depth)
    near_ref[...] = base_ref[pl.ds(start, depth)]
    far_ref[...] = base_ref[pl.ds(slab - depth - start, depth)]


def finish_base(sides, keep, found, after):
    _, slab, tall, lanes = keep.shape
    return pl.pallas_call(
        base_kernel,
        in_specs=[pl.BlockSpec(memory_space=pltpu.SMEM)]
        + [pl.BlockSpec(memory_space=pltpu.VMEM)] * 2
        + [pl.BlockSpec(memory_space=pl.ANY)] * len(after),
        out_specs=[pl.BlockSpec(memory_space=pltpu.VMEM)] * 3,
        out_shape=[jax.ShapeDtypeStruct((count, tall, lanes), jnp.float32) for count in (slab, 3, 3)],
        compiler_params=pltpu.CompilerParams(vmem_limit_bytes=SMALL_VMEM),
        cost_estimate=QUICK,
    )(sides, keep, found, *after)


def band_sum(sides, turns):
    count = lax.axis_size("freq")
    groups = [[i, i + 1] for i in range(0, count, 2)]
    send, keep = split(sides, lax.all_to_all(turns, "freq", 0, 0, axis_index_groups=groups, tiled=True))
    found = lax.ppermute(send, "freq", [(i, i ^ 2) for i in range(count)])
    return finish_base(sides, keep, found, [])


def local(saved_modes, mode_gains):
    _, modes, kinds, halves, parts, slab, rows, lanes = saved_modes.shape
    freqs = lax.axis_size("freq")
    slabs = lax.axis_size("space")
    factor = -2.0 / (saved_modes.shape[0] * freqs * modes)
    weights = (factor / 8.0) * mode_gains
    place = lax.axis_index("space")
    odd = place % 2
    near_pairs = [(i, i + 1) for i in range(0, slabs - 1, 2)]
    far_pairs = [(i, i + 1) for i in range(1, slabs - 1, 2)]

    def outer(plane, begin, count):
        start = (0, begin, 0, 0, 0, plane, 0, 0)
        found = lax.dynamic_slice(saved_modes, start, (1, count, kinds, halves, parts, 1, rows, lanes))
        return found.reshape((count, kinds, halves, parts, rows, lanes))

    last = modes - 1
    near_plane = jnp.where(odd == 0, slab - 1, 0)
    (far_out,) = planes(saved_modes, slab - 1 - near_plane, [(0, modes)], [])
    far_halo = swap(far_out, "space", far_pairs)
    near_out, last_out = planes(saved_modes, near_plane, [(0, last), (last, 1)], [far_out])
    near_halo = swap(near_out, "space", near_pairs)

    sides = jnp.stack([odd, lax.axis_index("freq")]).astype(jnp.int32)
    sens, near_edges, far_edges = interior(saved_modes, weights, sides, [near_out])
    base, near, far = band_sum(sides, finish_far(sides, weights, far_edges, far_halo, sens, freqs))
    near, far = swap(near, "space", near_pairs), swap(far, "space", far_pairs)
    where = jnp.stack([odd, place * slab, lax.axis_index("freq") * (rows // freqs)]).astype(jnp.int32)
    smoothed = smooth(where, base, near, far, slab * slabs, rows)

    last_halo = swap(last_out, "space", near_pairs)
    near_late, last_edges = near_part(weights, hbm(near_edges), hbm(near_halo), [base])
    near_late = finish_near(last, weights, last_edges, last_halo, near_late, 2 * freqs, [])
    return add_near(where, trade(near_late, near_pairs), smoothed, rows)


def solution(mesh):
    in_specs = (P("freq", None, None, None, None, "space", None, None), P("freq", None))
    out_specs = P("space", "freq", None)
    return jax.shard_map(local, mesh=mesh, in_specs=in_specs, out_specs=out_specs, check_vma=False)
```

```python
import functools

import jax
import jax.numpy as jnp
from jax import lax
from jax.experimental import pallas as pl
from jax.experimental.pallas import tpu as pltpu
from jax.sharding import PartitionSpec as P

AXIAL = 0.35
CROSS = 0.06
MARGIN = 8
EDGE = 4
STEP = 16
INTERIOR_VMEM = 30 * 1024 * 1024
QUICK = pl.CostEstimate(flops=1024, bytes_accessed=1024, transcendentals=0)
INTERIOR_FLOPS = 8 * 10**9
SMOOTH_FLOPS = 10**10
SMALL_VMEM = 16 * 1024 * 1024


def plane_kernel(begin, plane_ref, modes_ref, *refs):
    out_refs, sems = refs[-1 - len(begin) : -1], refs[-1]
    copies = []
    for at, (first, out_ref) in enumerate(zip(begin, out_refs, strict=True)):
        source = modes_ref.at[0, pl.ds(first, out_ref.shape[0]), :, :, :, plane_ref[0]]
        copies.append(pltpu.make_async_copy(source, out_ref, sems.at[at]))
        copies[-1].start()
    for copy in copies:
        copy.wait()


def planes(saved_modes, plane, groups, after):
    _, _, kinds, halves, parts, _, rows, lanes = saved_modes.shape
    return pl.pallas_call(
        functools.partial(plane_kernel, [first for first, _ in groups]),
        in_specs=[pl.BlockSpec(memory_space=pltpu.SMEM), pl.BlockSpec(memory_space=pl.ANY)]
        + [pl.BlockSpec(memory_space=pl.ANY)] * len(after),
        out_specs=[pl.BlockSpec(memory_space=pltpu.VMEM)] * len(groups),
        out_shape=[
            pltpu.VMEM((count, kinds, halves, parts, rows, lanes), saved_modes.dtype) for _, count in groups
        ],
        scratch_shapes=[pltpu.SemaphoreType.DMA((len(groups),))],
        compiler_params=pltpu.CompilerParams(vmem_limit_bytes=SMALL_VMEM),
        cost_estimate=QUICK,
    )(plane.reshape(1).astype(jnp.int32), hbm(saved_modes), *after)


def interior_kernel(begin, before, after, side_ref, weight_ref, modes_ref, *refs):
    sens_ref, token_ref, near_edge_ref, far_edge_ref, wide_ref, lane_ref = refs[before + after :]
    slab, rows, lanes = modes_ref.shape[2:]

    @pl.when((pl.program_id(0) == 0) & (pl.program_id(1) == 0))
    def _():
        sens_ref[...] = refs[0][...] if before else jnp.zeros_like(sens_ref)
        token_ref[...] = jnp.zeros_like(token_ref)
        for plane in (0, slab + 1):
            wide_ref[:, plane] = jnp.zeros_like(wide_ref[:, plane])
        for start in (0, MARGIN + rows):
            wide_ref[:, :, pl.ds(start, MARGIN)] = jnp.zeros_like(wide_ref[:, :, pl.ds(start, MARGIN)])

    source = lax.broadcasted_iota(jnp.int32, (lanes, lanes), 0)
    target = lax.broadcasted_iota(jnp.int32, (lanes, lanes), 1)
    difference = jnp.where(source == target + 1, 1.0, 0.0) - jnp.where(source == target - 1, 1.0, 0.0)
    difference = difference.astype(jnp.bfloat16)
    lane = lax.broadcasted_iota(jnp.int32, (STEP, lanes), 1)
    not_last = jnp.where(lane == lanes - 1, 0.0, 1.0)
    not_first = jnp.where(lane == 0, 0.0, 1.0)
    scale = weight_ref[0, begin + pl.program_id(0)]

    def load_plane(plane):
        for kind in range(2):
            for part in range(3):
                values = modes_ref[kind, part, plane]
                field = kind * 3 + part
                wide_ref[field, plane + 1, MARGIN : MARGIN + rows] = values.astype(jnp.float32)
                if part > 0:
                    lane_ref[field, plane] = jnp.dot(
                        values, difference, preferred_element_type=jnp.float32
                    )

    def terms(plane, start):
        sides = []
        for kind in range(2):

            def axial(part):
                field = kind * 3 + part
                return (
                    wide_ref[field, plane + 2, pl.ds(MARGIN + start, STEP)]
                    - wide_ref[field, plane, pl.ds(MARGIN + start, STEP)]
                )

            def by_row(part):
                field = kind * 3 + part
                return (
                    wide_ref[field, plane + 1, pl.ds(MARGIN + start + 1, STEP)]
                    - wide_ref[field, plane + 1, pl.ds(MARGIN + start - 1, STEP)]
                )

            def by_lane(part):
                if part > 0:
                    return lane_ref[kind * 3 + part, plane, pl.ds(start, STEP)]
                values = modes_ref[kind, part, plane, pl.ds(start, STEP)]
                upper = pltpu.roll(values, lanes - 1, 1).astype(jnp.float32)
                lower = pltpu.roll(values, 1, 1).astype(jnp.float32)
                return upper * not_last - lower * not_first

            outer = (axial(0), axial(1) + by_row(0), axial(2) + by_lane(0))
            inner = (by_row(1), by_lane(2), by_row(2) + by_lane(1))
            sides.append((outer, inner))
        return sides

    def inner_plane(plane):
        for start in range(0, rows, STEP):
            (ou, iu), (ov, iv) = terms(plane, start)
            diagonal = ou[0] * ov[0] + iu[0] * iv[0] + iu[1] * iv[1]
            mixed = ou[1] * ov[1] + ou[2] * ov[2] + iu[2] * iv[2]
            sens_ref[plane, pl.ds(MARGIN + start, STEP)] += scale * (2.0 * diagonal + mixed)

    def both(plane, carry):
        load_plane(plane + 1)
        inner_plane(plane)
        return carry

    load_plane(0)
    load_plane(1)
    lax.fori_loop(1, slab - 1, both, 0, unroll=True)

    odd = side_ref[0]
    near = (1 - odd) * (slab - 1)
    for edge_ref, plane, sign in (
        (near_edge_ref, near, 1.0 - 2.0 * odd.astype(jnp.float32)),
        (far_edge_ref, slab - 1 - near, 2.0 * odd.astype(jnp.float32) - 1.0),
    ):
        for start in range(0, rows, STEP):
            (ou, iu), (ov, iv) = terms(plane, start)
            diagonal = iu[0] * iv[0] + iu[1] * iv[1]
            mixed = iu[2] * iv[2]
            sens_ref[plane, pl.ds(MARGIN + start, STEP)] += scale * (2.0 * diagonal + mixed)
            for part in range(3):
                edge_ref[0, part, pl.ds(start, STEP)] = sign * ou[part]
                edge_ref[1, part, pl.ds(start, STEP)] = sign * ov[part]


def interior(saved_modes, weights, sides, begin, count, before, after):
    _, _, kinds, halves, parts, slab, rows, lanes = saved_modes.shape
    whole = (slab, rows + 2 * MARGIN, lanes)
    edges = (count, halves, kinds, parts, rows, lanes)
    fields = kinds * parts
    return pl.pallas_call(
        functools.partial(interior_kernel, begin, len(before), len(after)),
        grid=(count, halves),
        in_specs=[
            pl.BlockSpec(memory_space=pltpu.SMEM),
            pl.BlockSpec(memory_space=pltpu.SMEM),
            pl.BlockSpec(
                (None, None, kinds, None, parts, slab, rows, lanes),
                lambda m, c: (0, begin + m, 0, c, 0, 0, 0, 0),
            ),
        ]
        + [pl.BlockSpec(memory_space=pltpu.VMEM)] * len(before)
        + [pl.BlockSpec(memory_space=pl.ANY)] * len(after),
        out_specs=[
            pl.BlockSpec(whole, lambda m, c: (0, 0, 0)),
            pl.BlockSpec((8, lanes), lambda m, c: (0, 0)),
        ]
        + [pl.BlockSpec((None, None) + edges[2:], lambda m, c: (m, c, 0, 0, 0, 0))] * 2,
        out_shape=[
            pltpu.VMEM(whole, jnp.float32),
            jax.ShapeDtypeStruct((8, lanes), jnp.float32),
            pltpu.HBM(edges, jnp.float32),
            pltpu.VMEM(edges, jnp.float32),
        ],
        scratch_shapes=[
            pltpu.VMEM((fields, slab + 2, rows + 2 * MARGIN, lanes), jnp.float32),
            pltpu.VMEM((fields, slab, rows, lanes), jnp.float32),
        ],
        compiler_params=pltpu.CompilerParams(vmem_limit_bytes=INTERIOR_VMEM),
        cost_estimate=pl.CostEstimate(flops=INTERIOR_FLOPS, bytes_accessed=1024, transcendentals=0),
    )(sides, weights, saved_modes, *before, *after)


def strain_of(ref, mode):
    return lambda half, kind, part, start: ref[mode, half, kind, part, pl.ds(start, STEP)]


def halo_of(ref, mode):
    return lambda half, kind, part, start: ref[mode, kind, half, part, pl.ds(start, STEP)]


def outer_plane(start, shape, scales, strains, halos):
    halves, parts = shape
    total = None
    for scale, strain, halo in zip(scales, strains, halos, strict=True):
        found = None
        for half in range(halves):
            for part in range(parts):
                u, v = (
                    strain(half, kind, part, start) + halo(half, kind, part, start).astype(jnp.float32)
                    for kind in range(2)
                )
                term = u * v
                if part == 0:
                    term = 2.0 * term
                found = term if found is None else found + term
        found = scale * found
        total = found if total is None else total + found
    return total


def far_kernel(groups, side_ref, weight_ref, edge_ref, *refs):
    halo_refs = refs[:-3]
    sens_ref, turns_ref, tall_ref = refs[-3:]
    scales, strains, halos = [], [], []
    for (begin, count), halo_ref in zip(groups, halo_refs, strict=True):
        for mode in range(begin, begin + count):
            scales.append(weight_ref[0, mode])
            strains.append(strain_of(edge_ref, mode))
            halos.append(halo_of(halo_ref, mode - begin))
    slab = sens_ref.shape[0]
    _, halves, _, parts, rows, _ = edge_ref.shape
    count, _, tall, _ = turns_ref.shape
    band = tall - 2 * EDGE
    far = side_ref[0] * (slab - 1)
    tall_ref[...] = sens_ref[far]
    for start in range(0, rows, STEP):
        tall_ref[pl.ds(MARGIN + start, STEP)] += outer_plane(start, (halves, parts), scales, strains, halos)
    for piece in range(count):
        index, bits = 0, 1
        while bits < count:
            index = 2 * index + (piece // bits) % 2
            bits *= 2
        start = index * band + MARGIN - EDGE
        turns_ref[piece] = sens_ref[:, pl.ds(start, tall)]
        turns_ref[piece, far] = tall_ref[pl.ds(start, tall)]


def finish_far(sides, weights, groups, edges, halos, sens, freqs):
    slab, rows, lanes = sens.shape
    band = (rows - 2 * MARGIN) // freqs
    return pl.pallas_call(
        functools.partial(far_kernel, groups),
        in_specs=[pl.BlockSpec(memory_space=pltpu.SMEM)] * 2
        + [pl.BlockSpec(memory_space=pltpu.VMEM)] * (len(halos) + 2),
        out_specs=pl.BlockSpec(memory_space=pltpu.VMEM),
        out_shape=jax.ShapeDtypeStruct((freqs, slab, band + 2 * EDGE, lanes), jnp.float32),
        scratch_shapes=[pltpu.VMEM((rows, lanes), jnp.float32)],
        compiler_params=pltpu.CompilerParams(vmem_limit_bytes=SMALL_VMEM),
        cost_estimate=QUICK,
    )(sides, weights, edges, *halos, sens)


def fetch_kernel(count, *refs):
    sources, outs, sems = refs[:count], refs[-1 - count : -1], refs[-1]
    copies = [pltpu.make_async_copy(sources[i], outs[i], sems.at[i]) for i in range(count)]
    for copy in copies:
        copy.start()
    for copy in copies:
        copy.wait()


def fetch(blocks, after):
    return pl.pallas_call(
        functools.partial(fetch_kernel, len(blocks)),
        in_specs=[pl.BlockSpec(memory_space=pl.ANY)] * (len(blocks) + len(after)),
        out_specs=[pl.BlockSpec(memory_space=pltpu.VMEM)] * len(blocks),
        out_shape=[pltpu.VMEM(block.shape, block.dtype) for block in blocks],
        scratch_shapes=[pltpu.SemaphoreType.DMA((len(blocks),))],
        compiler_params=pltpu.CompilerParams(vmem_limit_bytes=SMALL_VMEM),
        cost_estimate=QUICK,
    )(*[hbm(block) for block in blocks], *after)


def near_kernel(weight_ref, edge_ref, halo_ref, out_ref, tall_ref, band_ref, done):
    modes, halves, _, parts, rows, _ = edge_ref.shape
    scales = [weight_ref[0, mode] for mode in range(modes)]
    strains = [strain_of(edge_ref, mode) for mode in range(modes)]
    halos = [halo_of(halo_ref, mode) for mode in range(modes)]
    pieces, tall, lanes = band_ref.shape
    band = tall - 2 * EDGE
    empty = jnp.zeros((MARGIN, lanes), jnp.float32)
    tall_ref[pl.ds(0, MARGIN)] = empty
    tall_ref[pl.ds(MARGIN + rows, MARGIN)] = empty
    for start in range(0, rows, STEP):
        tall_ref[pl.ds(MARGIN + start, STEP)] = outer_plane(start, (halves, parts), scales, strains, halos)
    for piece in range(pieces):
        band_ref[piece] = tall_ref[pl.ds(piece // 2 * band + MARGIN - EDGE, tall)]
    copy = pltpu.make_async_copy(band_ref, out_ref, done)
    copy.start()
    copy.wait()


def finish_near(weights, edges, halo, pieces):
    rows, lanes = halo.shape[4:]
    shape = (pieces, rows // (pieces // 2) + 2 * EDGE, lanes)
    return pl.pallas_call(
        near_kernel,
        in_specs=[pl.BlockSpec(memory_space=pltpu.SMEM)]
        + [pl.BlockSpec(memory_space=pltpu.VMEM)] * 2,
        out_specs=pl.BlockSpec(memory_space=pltpu.HBM),
        out_shape=pltpu.HBM(shape, jnp.float32),
        scratch_shapes=[
            pltpu.VMEM((rows + 2 * MARGIN, lanes), jnp.float32),
            pltpu.VMEM(shape, jnp.float32),
            pltpu.SemaphoreType.DMA(()),
        ],
        compiler_params=pltpu.CompilerParams(vmem_limit_bytes=SMALL_VMEM),
        cost_estimate=QUICK,
    )(weights, edges, halo)


class Pass:
    def __init__(self, tall, lanes, first_y, total_y):
        self.tall, self.lanes = tall, lanes
        self.lane = lax.broadcasted_iota(jnp.int32, (tall, lanes), 1)
        row = lax.broadcasted_iota(jnp.int32, (tall, lanes), 0) + (first_y - EDGE)
        self.inside = (row >= 0) & (row < total_y)

    def __call__(self, below, center, above):
        axial = above + below - 2.0 * center
        cross = (
            pltpu.roll(center, self.tall - 1, 0)
            + pltpu.roll(center, 1, 0)
            + jnp.where(self.lane == self.lanes - 1, 0.0, pltpu.roll(center, self.lanes - 1, 1))
            + jnp.where(self.lane == 0, 0.0, pltpu.roll(center, 1, 1))
            - 4.0 * center
        )
        return jnp.where(self.inside, center + AXIAL * axial + CROSS * cross, 0.0)


def smooth_kernel(total_x, total_y, place_ref, base_ref, near_ref, far_ref, out_ref, one_ref, two_ref):
    slab, tall, lanes = base_ref.shape
    first_x = place_ref[1]
    even = place_ref[0] == 0
    one_ref[pl.ds(3, slab)] = base_ref[...]
    near = near_ref[...]
    far = far_ref[...]
    one_ref[pl.ds(0, 3)] = jnp.where(even, far, near)
    one_ref[pl.ds(slab + 3, 3)] = jnp.where(even, near, far)
    smoothed = Pass(tall, lanes, place_ref[2], total_y)

    def clear(ref, plane):
        x = first_x + (plane - 3)

        @pl.when((x < 0) | (x >= total_x))
        def _():
            ref[plane] = jnp.zeros_like(ref[plane])

    def passed(source, plane):
        return smoothed(source[plane - 1], source[plane], source[plane + 1])

    for plane in range(1, slab + 5):
        two_ref[plane] = passed(one_ref, plane)
    for plane in (1, 2, slab + 3, slab + 4):
        clear(two_ref, plane)
    for plane in range(2, slab + 4):
        one_ref[plane] = passed(two_ref, plane)
    for plane in (2, slab + 3):
        clear(one_ref, plane)
    for plane in range(3, slab + 3):
        out_ref[plane - 3] = passed(one_ref, plane)[EDGE : tall - EDGE]


def smooth(place, base, near, far, total_x, total_y):
    slab, tall, lanes = base.shape
    return pl.pallas_call(
        functools.partial(smooth_kernel, total_x, total_y),
        in_specs=[pl.BlockSpec(memory_space=pltpu.SMEM)]
        + [pl.BlockSpec(memory_space=pltpu.VMEM)] * 3,
        out_specs=pl.BlockSpec(memory_space=pltpu.VMEM),
        out_shape=pltpu.VMEM((slab, tall - 2 * EDGE, lanes), jnp.float32),
        scratch_shapes=[pltpu.VMEM((slab + 6, tall, lanes), jnp.float32)] * 2,
        compiler_params=pltpu.CompilerParams(vmem_limit_bytes=SMALL_VMEM),
        cost_estimate=pl.CostEstimate(flops=SMOOTH_FLOPS, bytes_accessed=1024, transcendentals=0),
    )(place, base, near, far)


def add_near_kernel(total_y, place_ref, late_vmem, before_ref, out_ref):
    pieces, tall, lanes = late_vmem.shape
    slab, band = before_ref.shape[:2]
    even = place_ref[0] == 0
    first = jnp.where(even, slab - 4, 0)
    out_ref[...] = before_ref[...]
    smoothed = Pass(tall, lanes, place_ref[2], total_y)
    lower, upper = (
        functools.reduce(jnp.add, [late_vmem[i] for i in range(which, pieces, 2)]) for which in range(2)
    )
    zero = jnp.zeros_like(lower)
    planes = {-1: jnp.where(even, upper, lower), 0: jnp.where(even, lower, upper)}
    for reach in (1, 2, 3):
        low, high = max(-1 - reach, reach - 4), min(reach, 3)
        planes = {
            at: smoothed(planes.get(at - 1, zero), planes.get(at, zero), planes.get(at + 1, zero))
            for at in range(low, high + 1)
        }
    for at in range(4):
        out_ref[first + jnp.where(even, 3 - at, at)] += planes[at][EDGE : tall - EDGE]


def add_near(place, late, before, total_y):
    slab, band, lanes = before.shape
    return pl.pallas_call(
        functools.partial(add_near_kernel, total_y),
        in_specs=[pl.BlockSpec(memory_space=pltpu.SMEM)] + [pl.BlockSpec(memory_space=pltpu.VMEM)] * 2,
        out_specs=pl.BlockSpec(memory_space=pltpu.VMEM),
        out_shape=jax.ShapeDtypeStruct(before.shape, jnp.float32),
        compiler_params=pltpu.CompilerParams(vmem_limit_bytes=SMALL_VMEM),
        cost_estimate=QUICK,
    )(place, late, before)


def swap(block, axis, pairs):
    return lax.ppermute(block, axis, [p for a, b in pairs for p in ((a, b), (b, a))])


def trade(pieces, pairs):
    slabs = lax.axis_size("space")
    groups = [[f * slabs + s for f in range(lax.axis_size("freq")) for s in pair] for pair in pairs]
    return lax.all_to_all(pieces, ("freq", "space"), 0, 0, axis_index_groups=groups, tiled=True)


def hbm(block):
    return pltpu.with_memory_space_constraint(block, pltpu.HBM)


def split_kernel(side_ref, found_ref, send_ref, keep_ref):
    half = keep_ref.shape[0]
    which = side_ref[1] // 2 % 2
    for ref, side in ((keep_ref, which), (send_ref, 1 - which)):
        for piece in range(half):
            at = side * half + piece
            ref[piece] = found_ref[at] + found_ref[2 * half + at]


def split(sides, found):
    shape = (found.shape[0] // 4,) + found.shape[1:]
    return pl.pallas_call(
        split_kernel,
        in_specs=[pl.BlockSpec(memory_space=pltpu.SMEM), pl.BlockSpec(memory_space=pltpu.VMEM)],
        out_specs=[pl.BlockSpec(memory_space=pltpu.VMEM)] * 2,
        out_shape=[pltpu.VMEM(shape, jnp.float32)] * 2,
        compiler_params=pltpu.CompilerParams(vmem_limit_bytes=SMALL_VMEM),
        cost_estimate=QUICK,
    )(sides, found)


def base_kernel(side_ref, keep_ref, found_ref, *refs):
    base_ref, near_ref, far_ref = refs[-3:]
    slab, depth = base_ref.shape[0], near_ref.shape[0]
    base_ref[...] = keep_ref[0] + found_ref[0]
    start = (1 - side_ref[0]) * (slab - depth)
    near_ref[...] = base_ref[pl.ds(start, depth)]
    far_ref[...] = base_ref[pl.ds(slab - depth - start, depth)]


def finish_base(sides, keep, found, after):
    _, slab, tall, lanes = keep.shape
    return pl.pallas_call(
        base_kernel,
        in_specs=[pl.BlockSpec(memory_space=pltpu.SMEM)]
        + [pl.BlockSpec(memory_space=pltpu.VMEM)] * 2
        + [pl.BlockSpec(memory_space=pl.ANY)] * len(after),
        out_specs=[pl.BlockSpec(memory_space=pltpu.VMEM)] * 3,
        out_shape=[pltpu.VMEM((count, tall, lanes), jnp.float32) for count in (slab, 3, 3)],
        compiler_params=pltpu.CompilerParams(vmem_limit_bytes=SMALL_VMEM),
        cost_estimate=QUICK,
    )(sides, keep, found, *after)


def band_sum(sides, turns):
    count = lax.axis_size("freq")
    groups = [[i, i + 1] for i in range(0, count, 2)]
    send, keep = split(sides, lax.all_to_all(turns, "freq", 0, 0, axis_index_groups=groups, tiled=True))
    found = lax.ppermute(send, "freq", [(i, i ^ 2) for i in range(count)])
    return *finish_base(sides, keep, found, []), keep


def local(saved_modes, mode_gains):
    _, modes, kinds, halves, parts, slab, rows, lanes = saved_modes.shape
    freqs = lax.axis_size("freq")
    slabs = lax.axis_size("space")
    factor = -2.0 / (saved_modes.shape[0] * freqs * modes)
    weights = (factor / 8.0) * mode_gains
    place = lax.axis_index("space")
    odd = place % 2
    near_pairs = [(i, i + 1) for i in range(0, slabs - 1, 2)]
    far_pairs = [(i, i + 1) for i in range(1, slabs - 1, 2)]

    def outer(plane, begin, count):
        start = (0, begin, 0, 0, 0, plane, 0, 0)
        found = lax.dynamic_slice(saved_modes, start, (1, count, kinds, halves, parts, 1, rows, lanes))
        return found.reshape((count, kinds, halves, parts, rows, lanes))

    near_plane = jnp.where(odd == 0, slab - 1, 0)
    half = modes // 2
    groups = [(0, half), (half, modes - half)]
    (near_out,) = planes(saved_modes, near_plane, [(0, modes)], [])
    near_halo = swap(near_out, "space", near_pairs)
    far_outs = planes(saved_modes, slab - 1 - near_plane, groups, [near_out])
    far_halos = [swap(block, "space", far_pairs) for block in far_outs]

    sides = jnp.stack([odd, lax.axis_index("freq")]).astype(jnp.int32)
    sens, _, near_edges, far_edges = interior(saved_modes, weights, sides, 0, modes, [], far_outs)
    turns = finish_far(sides, weights, groups, far_edges, far_halos, sens, freqs)
    base, near, far, keep = band_sum(sides, turns)
    near, far = swap(near, "space", near_pairs), swap(far, "space", far_pairs)
    where = jnp.stack([odd, place * slab, lax.axis_index("freq") * (rows // freqs)]).astype(jnp.int32)
    smoothed = smooth(where, base, near, far, slab * slabs, rows)

    near_late = finish_near(weights, *fetch([near_edges], [keep]), near_halo, 2 * freqs)
    return add_near(where, trade(near_late, near_pairs), smoothed, rows)


def solution(mesh):
    in_specs = (P("freq", None, None, None, None, "space", None, None), P("freq", None))
    out_specs = P("space", "freq", None)
    return jax.shard_map(local, mesh=mesh, in_specs=in_specs, out_specs=out_specs, check_vma=False)
```

```python
import functools

import jax
import jax.numpy as jnp
from jax import lax
from jax.experimental import pallas as pl
from jax.experimental.pallas import tpu as pltpu
from jax.sharding import PartitionSpec as P

AXIAL = 0.35
CROSS = 0.06
MARGIN = 8
EDGE = 4
STEP = 16
INTERIOR_VMEM = 30 * 1024 * 1024
QUICK = pl.CostEstimate(flops=1024, bytes_accessed=1024, transcendentals=0)
INTERIOR_FLOPS = 8 * 10**9
SMOOTH_FLOPS = 10**10
SMALL_VMEM = 16 * 1024 * 1024


def plane_kernel(begin, plane_ref, modes_ref, *refs):
    out_refs, sems = refs[-1 - len(begin) : -1], refs[-1]
    copies = []
    for at, (first, out_ref) in enumerate(zip(begin, out_refs, strict=True)):
        source = modes_ref.at[0, pl.ds(first, out_ref.shape[0]), :, :, :, plane_ref[0]]
        copies.append(pltpu.make_async_copy(source, out_ref, sems.at[at]))
        copies[-1].start()
    for copy in copies:
        copy.wait()


def planes(saved_modes, plane, groups, after):
    _, _, kinds, halves, parts, _, rows, lanes = saved_modes.shape
    return pl.pallas_call(
        functools.partial(plane_kernel, [first for first, _ in groups]),
        in_specs=[pl.BlockSpec(memory_space=pltpu.SMEM), pl.BlockSpec(memory_space=pl.ANY)]
        + [pl.BlockSpec(memory_space=pl.ANY)] * len(after),
        out_specs=[pl.BlockSpec(memory_space=pltpu.VMEM)] * len(groups),
        out_shape=[
            pltpu.VMEM((count, kinds, halves, parts, rows, lanes), saved_modes.dtype) for _, count in groups
        ],
        scratch_shapes=[pltpu.SemaphoreType.DMA((len(groups),))],
        compiler_params=pltpu.CompilerParams(vmem_limit_bytes=SMALL_VMEM),
        cost_estimate=QUICK,
    )(plane.reshape(1).astype(jnp.int32), hbm(saved_modes), *after)


def interior_kernel(begin, before, after, side_ref, weight_ref, modes_ref, *refs):
    sens_ref, token_ref, near_edge_ref, far_edge_ref, wide_ref, lane_ref = refs[before + after :]
    slab, rows, lanes = modes_ref.shape[2:]

    @pl.when((pl.program_id(0) == 0) & (pl.program_id(1) == 0))
    def _():
        sens_ref[...] = refs[0][...] if before else jnp.zeros_like(sens_ref)
        token_ref[...] = jnp.zeros_like(token_ref)
        for plane in (0, slab + 1):
            wide_ref[:, plane] = jnp.zeros_like(wide_ref[:, plane])
        for start in (0, MARGIN + rows):
            wide_ref[:, :, pl.ds(start, MARGIN)] = jnp.zeros_like(wide_ref[:, :, pl.ds(start, MARGIN)])

    source = lax.broadcasted_iota(jnp.int32, (lanes, lanes), 0)
    target = lax.broadcasted_iota(jnp.int32, (lanes, lanes), 1)
    difference = jnp.where(source == target + 1, 1.0, 0.0) - jnp.where(source == target - 1, 1.0, 0.0)
    difference = difference.astype(jnp.bfloat16)
    lane = lax.broadcasted_iota(jnp.int32, (STEP, lanes), 1)
    not_last = jnp.where(lane == lanes - 1, 0.0, 1.0)
    not_first = jnp.where(lane == 0, 0.0, 1.0)
    scale = weight_ref[0, begin + pl.program_id(0)]

    def load_plane(plane):
        for kind in range(2):
            for part in range(3):
                values = modes_ref[kind, part, plane]
                field = kind * 3 + part
                wide_ref[field, plane + 1, MARGIN : MARGIN + rows] = values.astype(jnp.float32)
                if part > 0:
                    lane_ref[field, plane] = jnp.dot(
                        values, difference, preferred_element_type=jnp.float32
                    )

    def terms(plane, start):
        sides = []
        for kind in range(2):

            def axial(part):
                field = kind * 3 + part
                return (
                    wide_ref[field, plane + 2, pl.ds(MARGIN + start, STEP)]
                    - wide_ref[field, plane, pl.ds(MARGIN + start, STEP)]
                )

            def by_row(part):
                field = kind * 3 + part
                return (
                    wide_ref[field, plane + 1, pl.ds(MARGIN + start + 1, STEP)]
                    - wide_ref[field, plane + 1, pl.ds(MARGIN + start - 1, STEP)]
                )

            def by_lane(part):
                if part > 0:
                    return lane_ref[kind * 3 + part, plane, pl.ds(start, STEP)]
                values = modes_ref[kind, part, plane, pl.ds(start, STEP)]
                upper = pltpu.roll(values, lanes - 1, 1).astype(jnp.float32)
                lower = pltpu.roll(values, 1, 1).astype(jnp.float32)
                return upper * not_last - lower * not_first

            outer = (axial(0), axial(1) + by_row(0), axial(2) + by_lane(0))
            inner = (by_row(1), by_lane(2), by_row(2) + by_lane(1))
            sides.append((outer, inner))
        return sides

    def inner_plane(plane):
        for start in range(0, rows, STEP):
            (ou, iu), (ov, iv) = terms(plane, start)
            diagonal = ou[0] * ov[0] + iu[0] * iv[0] + iu[1] * iv[1]
            mixed = ou[1] * ov[1] + ou[2] * ov[2] + iu[2] * iv[2]
            sens_ref[plane, pl.ds(MARGIN + start, STEP)] += scale * (2.0 * diagonal + mixed)

    def both(plane, carry):
        load_plane(plane + 1)
        inner_plane(plane)
        return carry

    load_plane(0)
    load_plane(1)
    lax.fori_loop(1, slab - 1, both, 0, unroll=True)

    odd = side_ref[0]
    near = (1 - odd) * (slab - 1)
    for edge_ref, plane, sign in (
        (near_edge_ref, near, 1.0 - 2.0 * odd.astype(jnp.float32)),
        (far_edge_ref, slab - 1 - near, 2.0 * odd.astype(jnp.float32) - 1.0),
    ):
        for start in range(0, rows, STEP):
            (ou, iu), (ov, iv) = terms(plane, start)
            diagonal = iu[0] * iv[0] + iu[1] * iv[1]
            mixed = iu[2] * iv[2]
            sens_ref[plane, pl.ds(MARGIN + start, STEP)] += scale * (2.0 * diagonal + mixed)
            for part in range(3):
                edge_ref[0, part, pl.ds(start, STEP)] = sign * ou[part]
                edge_ref[1, part, pl.ds(start, STEP)] = sign * ov[part]


def interior(saved_modes, weights, sides, begin, count, before, after):
    _, _, kinds, halves, parts, slab, rows, lanes = saved_modes.shape
    whole = (slab, rows + 2 * MARGIN, lanes)
    edges = (count, halves, kinds, parts, rows, lanes)
    fields = kinds * parts
    return pl.pallas_call(
        functools.partial(interior_kernel, begin, len(before), len(after)),
        grid=(count, halves),
        in_specs=[
            pl.BlockSpec(memory_space=pltpu.SMEM),
            pl.BlockSpec(memory_space=pltpu.SMEM),
            pl.BlockSpec(
                (None, None, kinds, None, parts, slab, rows, lanes),
                lambda m, c: (0, begin + m, 0, c, 0, 0, 0, 0),
            ),
        ]
        + [pl.BlockSpec(memory_space=pltpu.VMEM)] * len(before)
        + [pl.BlockSpec(memory_space=pl.ANY)] * len(after),
        out_specs=[
            pl.BlockSpec(whole, lambda m, c: (0, 0, 0)),
            pl.BlockSpec((8, lanes), lambda m, c: (0, 0)),
        ]
        + [pl.BlockSpec((None, None) + edges[2:], lambda m, c: (m, c, 0, 0, 0, 0))] * 2,
        out_shape=[
            pltpu.VMEM(whole, jnp.float32),
            jax.ShapeDtypeStruct((8, lanes), jnp.float32),
            pltpu.HBM(edges, jnp.float32),
            pltpu.VMEM(edges, jnp.float32),
        ],
        scratch_shapes=[
            pltpu.VMEM((fields, slab + 2, rows + 2 * MARGIN, lanes), jnp.float32),
            pltpu.VMEM((fields, slab, rows, lanes), jnp.float32),
        ],
        compiler_params=pltpu.CompilerParams(vmem_limit_bytes=INTERIOR_VMEM),
        cost_estimate=pl.CostEstimate(flops=INTERIOR_FLOPS, bytes_accessed=1024, transcendentals=0),
    )(sides, weights, saved_modes, *before, *after)


def strain_of(ref, mode):
    return lambda half, kind, part, start: ref[mode, half, kind, part, pl.ds(start, STEP)]


def halo_of(ref, mode):
    return lambda half, kind, part, start: ref[mode, kind, half, part, pl.ds(start, STEP)]


def outer_plane(start, shape, scales, strains, halos):
    halves, parts = shape
    total = None
    for scale, strain, halo in zip(scales, strains, halos, strict=True):
        found = None
        for half in range(halves):
            for part in range(parts):
                u, v = (
                    strain(half, kind, part, start) + halo(half, kind, part, start).astype(jnp.float32)
                    for kind in range(2)
                )
                term = u * v
                if part == 0:
                    term = 2.0 * term
                found = term if found is None else found + term
        found = scale * found
        total = found if total is None else total + found
    return total


def far_kernel(groups, side_ref, weight_ref, edge_ref, *refs):
    halo_refs = refs[:-3]
    sens_ref, turns_ref, tall_ref = refs[-3:]
    scales, strains, halos = [], [], []
    for (begin, count), halo_ref in zip(groups, halo_refs, strict=True):
        for mode in range(begin, begin + count):
            scales.append(weight_ref[0, mode])
            strains.append(strain_of(edge_ref, mode))
            halos.append(halo_of(halo_ref, mode - begin))
    slab = sens_ref.shape[0]
    _, halves, _, parts, rows, _ = edge_ref.shape
    count, _, tall, _ = turns_ref.shape
    band = tall - 2 * EDGE
    far = side_ref[0] * (slab - 1)
    tall_ref[...] = sens_ref[far]
    for start in range(0, rows, STEP):
        tall_ref[pl.ds(MARGIN + start, STEP)] += outer_plane(start, (halves, parts), scales, strains, halos)
    for piece in range(count):
        index, bits = 0, 1
        while bits < count:
            index = 2 * index + (piece // bits) % 2
            bits *= 2
        start = index * band + MARGIN - EDGE
        turns_ref[piece] = sens_ref[:, pl.ds(start, tall)]
        turns_ref[piece, far] = tall_ref[pl.ds(start, tall)]


def finish_far(sides, weights, groups, edges, halos, sens, freqs):
    slab, rows, lanes = sens.shape
    band = (rows - 2 * MARGIN) // freqs
    return pl.pallas_call(
        functools.partial(far_kernel, groups),
        in_specs=[pl.BlockSpec(memory_space=pltpu.SMEM)] * 2
        + [pl.BlockSpec(memory_space=pltpu.VMEM)] * (len(halos) + 2),
        out_specs=pl.BlockSpec(memory_space=pltpu.VMEM),
        out_shape=jax.ShapeDtypeStruct((freqs, slab, band + 2 * EDGE, lanes), jnp.float32),
        scratch_shapes=[pltpu.VMEM((rows, lanes), jnp.float32)],
        compiler_params=pltpu.CompilerParams(vmem_limit_bytes=SMALL_VMEM),
        cost_estimate=QUICK,
    )(sides, weights, edges, *halos, sens)


def fetch_kernel(count, *refs):
    sources, outs, sems = refs[:count], refs[-1 - count : -1], refs[-1]
    copies = [pltpu.make_async_copy(sources[i], outs[i], sems.at[i]) for i in range(count)]
    for copy in copies:
        copy.start()
    for copy in copies:
        copy.wait()


def fetch(blocks, after):
    return pl.pallas_call(
        functools.partial(fetch_kernel, len(blocks)),
        in_specs=[pl.BlockSpec(memory_space=pl.ANY)] * (len(blocks) + len(after)),
        out_specs=[pl.BlockSpec(memory_space=pltpu.VMEM)] * len(blocks),
        out_shape=[pltpu.VMEM(block.shape, block.dtype) for block in blocks],
        scratch_shapes=[pltpu.SemaphoreType.DMA((len(blocks),))],
        compiler_params=pltpu.CompilerParams(vmem_limit_bytes=SMALL_VMEM),
        cost_estimate=QUICK,
    )(*[hbm(block) for block in blocks], *after)


def near_kernel(side_ref, weight_ref, edge_ref, halo_ref, keep_ref, give_ref, tall_ref):
    modes, halves, _, parts, rows, _ = edge_ref.shape
    scales = [weight_ref[0, mode] for mode in range(modes)]
    strains = [strain_of(edge_ref, mode) for mode in range(modes)]
    halos = [halo_of(halo_ref, mode) for mode in range(modes)]
    _, tall, lanes = keep_ref.shape
    band = tall - 2 * EDGE
    empty = jnp.zeros((2 * EDGE, lanes), jnp.float32)
    tall_ref[pl.ds(0, 2 * EDGE)] = empty
    tall_ref[pl.ds(rows, 2 * EDGE)] = empty
    for start in range(0, rows, STEP):
        tall_ref[pl.ds(EDGE + start, STEP)] = outer_plane(start, (halves, parts), scales, strains, halos)
    for turn, ref in enumerate((keep_ref, give_ref, keep_ref, give_ref)):
        start = pl.multiple_of((side_ref[1] ^ turn) * band, 8)
        ref[turn // 2] = tall_ref[pl.ds(start, tall)]


def finish_near(sides, weights, edges, halo, freqs):
    rows, lanes = edges.shape[4:]
    bands = jax.ShapeDtypeStruct((2, rows // freqs + 2 * EDGE, lanes), jnp.float32)
    return pl.pallas_call(
        near_kernel,
        in_specs=[pl.BlockSpec(memory_space=pltpu.SMEM)] * 2 + [pl.BlockSpec(memory_space=pltpu.VMEM)] * 2,
        out_specs=[pl.BlockSpec(memory_space=pltpu.VMEM)] * 2,
        out_shape=[bands] * 2,
        scratch_shapes=[pltpu.VMEM((rows + 2 * EDGE, lanes), jnp.float32)],
        compiler_params=pltpu.CompilerParams(vmem_limit_bytes=SMALL_VMEM),
        cost_estimate=QUICK,
    )(sides, weights, edges, halo)


def pair_kernel(keep_ref, found_ref, own_ref, other_ref):
    own_ref[...] = keep_ref[0] + found_ref[0]
    other_ref[...] = keep_ref[1] + found_ref[1]


def pair_sum(keep, found):
    band = jax.ShapeDtypeStruct(keep.shape[1:], jnp.float32)
    return pl.pallas_call(
        pair_kernel,
        in_specs=[pl.BlockSpec(memory_space=pltpu.VMEM)] * 2,
        out_specs=[pl.BlockSpec(memory_space=pltpu.VMEM)] * 2,
        out_shape=[band] * 2,
        compiler_params=pltpu.CompilerParams(vmem_limit_bytes=SMALL_VMEM),
        cost_estimate=QUICK,
    )(keep, found)


class Pass:
    def __init__(self, tall, lanes, first_y, total_y):
        self.tall, self.lanes = tall, lanes
        self.lane = lax.broadcasted_iota(jnp.int32, (tall, lanes), 1)
        row = lax.broadcasted_iota(jnp.int32, (tall, lanes), 0) + (first_y - EDGE)
        self.inside = (row >= 0) & (row < total_y)

    def __call__(self, below, center, above):
        axial = above + below - 2.0 * center
        cross = (
            pltpu.roll(center, self.tall - 1, 0)
            + pltpu.roll(center, 1, 0)
            + jnp.where(self.lane == self.lanes - 1, 0.0, pltpu.roll(center, self.lanes - 1, 1))
            + jnp.where(self.lane == 0, 0.0, pltpu.roll(center, 1, 1))
            - 4.0 * center
        )
        return jnp.where(self.inside, center + AXIAL * axial + CROSS * cross, 0.0)


def smooth_kernel(total_x, total_y, place_ref, base_ref, near_ref, far_ref, out_ref, one_ref, two_ref):
    slab, tall, lanes = base_ref.shape
    first_x = place_ref[1]
    even = place_ref[0] == 0
    one_ref[pl.ds(3, slab)] = base_ref[...]
    near = near_ref[...]
    far = far_ref[...]
    one_ref[pl.ds(0, 3)] = jnp.where(even, far, near)
    one_ref[pl.ds(slab + 3, 3)] = jnp.where(even, near, far)
    smoothed = Pass(tall, lanes, place_ref[2], total_y)

    def clear(ref, plane):
        x = first_x + (plane - 3)

        @pl.when((x < 0) | (x >= total_x))
        def _():
            ref[plane] = jnp.zeros_like(ref[plane])

    def passed(source, plane):
        return smoothed(source[plane - 1], source[plane], source[plane + 1])

    for plane in range(1, slab + 5):
        two_ref[plane] = passed(one_ref, plane)
    for plane in (1, 2, slab + 3, slab + 4):
        clear(two_ref, plane)
    for plane in range(2, slab + 4):
        one_ref[plane] = passed(two_ref, plane)
    for plane in (2, slab + 3):
        clear(one_ref, plane)
    for plane in range(3, slab + 3):
        out_ref[plane - 3] = passed(one_ref, plane)[EDGE : tall - EDGE]


def smooth(place, base, near, far, total_x, total_y):
    slab, tall, lanes = base.shape
    return pl.pallas_call(
        functools.partial(smooth_kernel, total_x, total_y),
        in_specs=[pl.BlockSpec(memory_space=pltpu.SMEM)]
        + [pl.BlockSpec(memory_space=pltpu.VMEM)] * 3,
        out_specs=pl.BlockSpec(memory_space=pltpu.VMEM),
        out_shape=pltpu.VMEM((slab, tall - 2 * EDGE, lanes), jnp.float32),
        scratch_shapes=[pltpu.VMEM((slab + 6, tall, lanes), jnp.float32)] * 2,
        compiler_params=pltpu.CompilerParams(vmem_limit_bytes=SMALL_VMEM),
        cost_estimate=pl.CostEstimate(flops=SMOOTH_FLOPS, bytes_accessed=1024, transcendentals=0),
    )(place, base, near, far)


def add_near_kernel(total_y, place_ref, own_refs, beyond_refs, before_ref, out_ref):
    tall, lanes = own_refs[0].shape
    slab = before_ref.shape[0]
    even = place_ref[0] == 0
    first = jnp.where(even, slab - 4, 0)
    out_ref[...] = before_ref[...]
    smoothed = Pass(tall, lanes, place_ref[2], total_y)
    own, beyond = (refs[0][...] + refs[1][...] for refs in (own_refs, beyond_refs))
    zero = jnp.zeros_like(own)
    planes = {-1: beyond, 0: own}
    for reach in (1, 2, 3):
        low, high = max(-1 - reach, reach - 4), min(reach, 3)
        planes = {
            at: smoothed(planes.get(at - 1, zero), planes.get(at, zero), planes.get(at + 1, zero))
            for at in range(low, high + 1)
        }
    for at in range(4):
        out_ref[first + jnp.where(even, 3 - at, at)] += planes[at][EDGE : tall - EDGE]


def add_near(place, own, beyond, before, total_y):
    slab, band, lanes = before.shape
    return pl.pallas_call(
        functools.partial(add_near_kernel, total_y),
        in_specs=[pl.BlockSpec(memory_space=pltpu.SMEM)]
        + [[pl.BlockSpec(memory_space=pltpu.VMEM)] * 2] * 2
        + [pl.BlockSpec(memory_space=pltpu.VMEM)],
        out_specs=pl.BlockSpec(memory_space=pltpu.VMEM),
        out_shape=jax.ShapeDtypeStruct(before.shape, jnp.float32),
        compiler_params=pltpu.CompilerParams(vmem_limit_bytes=SMALL_VMEM),
        cost_estimate=QUICK,
    )(place, own, beyond, before)


def swap(block, axis, pairs):
    return lax.ppermute(block, axis, [p for a, b in pairs for p in ((a, b), (b, a))])


def both(freq_pairs, space_pairs, slabs):
    return [(f * slabs + s, g * slabs + r) for f, g in freq_pairs for s, r in space_pairs]


def near_sums(keep, give, near_pairs):
    freqs, slabs = lax.axis_size("freq"), lax.axis_size("space")
    own, other = pair_sum(keep, lax.ppermute(give, "freq", [(i, i ^ 1) for i in range(freqs)]))
    across = [(i, i ^ 2) for i in range(freqs)]
    swaps = [p for a, b in near_pairs for p in ((a, b), (b, a))]
    from_own = lax.ppermute(other, "freq", across)
    beyond = lax.ppermute(own, "space", swaps)
    from_beyond = lax.ppermute(other, ("freq", "space"), both(across, swaps, slabs))
    return [own, from_own], [beyond, from_beyond]


def hbm(block):
    return pltpu.with_memory_space_constraint(block, pltpu.HBM)


def split_kernel(side_ref, found_ref, send_ref, keep_ref):
    half = keep_ref.shape[0]
    which = side_ref[1] // 2 % 2
    for ref, side in ((keep_ref, which), (send_ref, 1 - which)):
        for piece in range(half):
            at = side * half + piece
            ref[piece] = found_ref[at] + found_ref[2 * half + at]


def split(sides, found):
    shape = (found.shape[0] // 4,) + found.shape[1:]
    return pl.pallas_call(
        split_kernel,
        in_specs=[pl.BlockSpec(memory_space=pltpu.SMEM), pl.BlockSpec(memory_space=pltpu.VMEM)],
        out_specs=[pl.BlockSpec(memory_space=pltpu.VMEM)] * 2,
        out_shape=[pltpu.VMEM(shape, jnp.float32)] * 2,
        compiler_params=pltpu.CompilerParams(vmem_limit_bytes=SMALL_VMEM),
        cost_estimate=QUICK,
    )(sides, found)


def base_kernel(side_ref, keep_ref, found_ref, *refs):
    base_ref, near_ref, far_ref = refs[-3:]
    slab, depth = base_ref.shape[0], near_ref.shape[0]
    base_ref[...] = keep_ref[0] + found_ref[0]
    start = (1 - side_ref[0]) * (slab - depth)
    near_ref[...] = base_ref[pl.ds(start, depth)]
    far_ref[...] = base_ref[pl.ds(slab - depth - start, depth)]


def finish_base(sides, keep, found, after):
    _, slab, tall, lanes = keep.shape
    return pl.pallas_call(
        base_kernel,
        in_specs=[pl.BlockSpec(memory_space=pltpu.SMEM)]
        + [pl.BlockSpec(memory_space=pltpu.VMEM)] * 2
        + [pl.BlockSpec(memory_space=pl.ANY)] * len(after),
        out_specs=[pl.BlockSpec(memory_space=pltpu.VMEM)] * 3,
        out_shape=[pltpu.VMEM((count, tall, lanes), jnp.float32) for count in (slab, 3, 3)],
        compiler_params=pltpu.CompilerParams(vmem_limit_bytes=SMALL_VMEM),
        cost_estimate=QUICK,
    )(sides, keep, found, *after)


def band_sum(sides, turns):
    count = lax.axis_size("freq")
    groups = [[i, i + 1] for i in range(0, count, 2)]
    send, keep = split(sides, lax.all_to_all(turns, "freq", 0, 0, axis_index_groups=groups, tiled=True))
    found = lax.ppermute(send, "freq", [(i, i ^ 2) for i in range(count)])
    return *finish_base(sides, keep, found, []), keep


def local(saved_modes, mode_gains):
    _, modes, kinds, halves, parts, slab, rows, lanes = saved_modes.shape
    freqs = lax.axis_size("freq")
    slabs = lax.axis_size("space")
    factor = -2.0 / (saved_modes.shape[0] * freqs * modes)
    weights = (factor / 8.0) * mode_gains
    place = lax.axis_index("space")
    odd = place % 2
    near_pairs = [(i, i + 1) for i in range(0, slabs - 1, 2)]
    far_pairs = [(i, i + 1) for i in range(1, slabs - 1, 2)]

    def outer(plane, begin, count):
        start = (0, begin, 0, 0, 0, plane, 0, 0)
        found = lax.dynamic_slice(saved_modes, start, (1, count, kinds, halves, parts, 1, rows, lanes))
        return found.reshape((count, kinds, halves, parts, rows, lanes))

    near_plane = jnp.where(odd == 0, slab - 1, 0)
    half = modes // 2
    groups = [(0, half), (half, modes - half)]
    (near_out,) = planes(saved_modes, near_plane, [(0, modes)], [])
    near_halo = swap(near_out, "space", near_pairs)
    far_outs = planes(saved_modes, slab - 1 - near_plane, groups, [near_out])
    far_halos = [swap(block, "space", far_pairs) for block in far_outs]

    sides = jnp.stack([odd, lax.axis_index("freq")]).astype(jnp.int32)
    sens, _, near_edges, far_edges = interior(saved_modes, weights, sides, 0, modes, [], far_outs)
    turns = finish_far(sides, weights, groups, far_edges, far_halos, sens, freqs)
    base, near, far, keep = band_sum(sides, turns)
    near, far = swap(near, "space", near_pairs), swap(far, "space", far_pairs)
    where = jnp.stack([odd, place * slab, lax.axis_index("freq") * (rows // freqs)]).astype(jnp.int32)
    smoothed = smooth(where, base, near, far, slab * slabs, rows)

    keep, give = finish_near(sides, weights, *fetch([near_edges], [keep]), near_halo, freqs)
    return add_near(where, *near_sums(keep, give, near_pairs), smoothed, rows)


def solution(mesh):
    in_specs = (P("freq", None, None, None, None, "space", None, None), P("freq", None))
    out_specs = P("space", "freq", None)
    return jax.shard_map(local, mesh=mesh, in_specs=in_specs, out_specs=out_specs, check_vma=False)
```

```python
import functools

import jax
import jax.numpy as jnp
from jax import lax
from jax.experimental import pallas as pl
from jax.experimental.pallas import tpu as pltpu
from jax.sharding import PartitionSpec as P

AXIAL = 0.35
CROSS = 0.06
MARGIN = 8
EDGE = 4
STEP = 16
INTERIOR_VMEM = 30 * 1024 * 1024
QUICK = pl.CostEstimate(flops=1024, bytes_accessed=1024, transcendentals=0)
INTERIOR_FLOPS = 8 * 10**9
SMOOTH_FLOPS = 10**10
SMALL_VMEM = 16 * 1024 * 1024


def plane_kernel(begin, plane_ref, modes_ref, *refs):
    out_refs, sems = refs[-1 - len(begin) : -1], refs[-1]
    copies = []
    for at, (first, out_ref) in enumerate(zip(begin, out_refs, strict=True)):
        source = modes_ref.at[0, pl.ds(first, out_ref.shape[0]), :, :, :, plane_ref[0]]
        copies.append(pltpu.make_async_copy(source, out_ref, sems.at[at]))
        copies[-1].start()
    for copy in copies:
        copy.wait()


def planes(saved_modes, plane, groups, after):
    _, _, kinds, halves, parts, _, rows, lanes = saved_modes.shape
    return pl.pallas_call(
        functools.partial(plane_kernel, [first for first, _ in groups]),
        in_specs=[pl.BlockSpec(memory_space=pltpu.SMEM), pl.BlockSpec(memory_space=pl.ANY)]
        + [pl.BlockSpec(memory_space=pl.ANY)] * len(after),
        out_specs=[pl.BlockSpec(memory_space=pltpu.VMEM)] * len(groups),
        out_shape=[
            pltpu.VMEM((count, kinds, halves, parts, rows, lanes), saved_modes.dtype) for _, count in groups
        ],
        scratch_shapes=[pltpu.SemaphoreType.DMA((len(groups),))],
        compiler_params=pltpu.CompilerParams(vmem_limit_bytes=SMALL_VMEM),
        cost_estimate=QUICK,
    )(plane.reshape(1).astype(jnp.int32), hbm(saved_modes), *after)


def interior_kernel(begin, before, after, side_ref, weight_ref, modes_ref, *refs):
    sens_ref, token_ref, near_edge_ref, far_edge_ref, wide_ref, lane_ref = refs[before + after :]
    slab, rows, lanes = modes_ref.shape[2:]

    @pl.when((pl.program_id(0) == 0) & (pl.program_id(1) == 0))
    def _():
        sens_ref[...] = refs[0][...] if before else jnp.zeros_like(sens_ref)
        token_ref[...] = jnp.zeros_like(token_ref)
        for plane in (0, slab + 1):
            wide_ref[:, plane] = jnp.zeros_like(wide_ref[:, plane])
        for start in (0, MARGIN + rows):
            wide_ref[:, :, pl.ds(start, MARGIN)] = jnp.zeros_like(wide_ref[:, :, pl.ds(start, MARGIN)])

    source = lax.broadcasted_iota(jnp.int32, (lanes, lanes), 0)
    target = lax.broadcasted_iota(jnp.int32, (lanes, lanes), 1)
    difference = jnp.where(source == target + 1, 1.0, 0.0) - jnp.where(source == target - 1, 1.0, 0.0)
    difference = difference.astype(jnp.bfloat16)
    lane = lax.broadcasted_iota(jnp.int32, (STEP, lanes), 1)
    not_last = jnp.where(lane == lanes - 1, 0.0, 1.0)
    not_first = jnp.where(lane == 0, 0.0, 1.0)
    scale = weight_ref[0, begin + pl.program_id(0)]

    def load_plane(plane):
        for kind in range(2):
            for part in range(3):
                values = modes_ref[kind, part, plane]
                field = kind * 3 + part
                wide_ref[field, plane + 1, MARGIN : MARGIN + rows] = values.astype(jnp.float32)
                if part > 0:
                    lane_ref[field, plane] = jnp.dot(
                        values, difference, preferred_element_type=jnp.float32
                    )

    def terms(plane, start):
        sides = []
        for kind in range(2):

            def axial(part):
                field = kind * 3 + part
                return (
                    wide_ref[field, plane + 2, pl.ds(MARGIN + start, STEP)]
                    - wide_ref[field, plane, pl.ds(MARGIN + start, STEP)]
                )

            def by_row(part):
                field = kind * 3 + part
                return (
                    wide_ref[field, plane + 1, pl.ds(MARGIN + start + 1, STEP)]
                    - wide_ref[field, plane + 1, pl.ds(MARGIN + start - 1, STEP)]
                )

            def by_lane(part):
                if part > 0:
                    return lane_ref[kind * 3 + part, plane, pl.ds(start, STEP)]
                values = modes_ref[kind, part, plane, pl.ds(start, STEP)]
                upper = pltpu.roll(values, lanes - 1, 1).astype(jnp.float32)
                lower = pltpu.roll(values, 1, 1).astype(jnp.float32)
                return upper * not_last - lower * not_first

            outer = (axial(0), axial(1) + by_row(0), axial(2) + by_lane(0))
            inner = (by_row(1), by_lane(2), by_row(2) + by_lane(1))
            sides.append((outer, inner))
        return sides

    def inner_plane(plane):
        for start in range(0, rows, STEP):
            (ou, iu), (ov, iv) = terms(plane, start)
            diagonal = ou[0] * ov[0] + iu[0] * iv[0] + iu[1] * iv[1]
            mixed = ou[1] * ov[1] + ou[2] * ov[2] + iu[2] * iv[2]
            sens_ref[plane, pl.ds(MARGIN + start, STEP)] += scale * (2.0 * diagonal + mixed)

    def both(plane, carry):
        load_plane(plane + 1)
        inner_plane(plane)
        return carry

    load_plane(0)
    load_plane(1)
    lax.fori_loop(1, slab - 1, both, 0, unroll=True)

    odd = side_ref[0]
    near = (1 - odd) * (slab - 1)
    for edge_ref, plane, sign in (
        (near_edge_ref, near, 1.0 - 2.0 * odd.astype(jnp.float32)),
        (far_edge_ref, slab - 1 - near, 2.0 * odd.astype(jnp.float32) - 1.0),
    ):
        for start in range(0, rows, STEP):
            (ou, iu), (ov, iv) = terms(plane, start)
            diagonal = iu[0] * iv[0] + iu[1] * iv[1]
            mixed = iu[2] * iv[2]
            sens_ref[plane, pl.ds(MARGIN + start, STEP)] += scale * (2.0 * diagonal + mixed)
            for part in range(3):
                edge_ref[0, part, pl.ds(start, STEP)] = sign * ou[part]
                edge_ref[1, part, pl.ds(start, STEP)] = sign * ov[part]


def interior(saved_modes, weights, sides, begin, count, before, after):
    _, _, kinds, halves, parts, slab, rows, lanes = saved_modes.shape
    whole = (slab, rows + 2 * MARGIN, lanes)
    edges = (count, halves, kinds, parts, rows, lanes)
    fields = kinds * parts
    return pl.pallas_call(
        functools.partial(interior_kernel, begin, len(before), len(after)),
        grid=(count, halves),
        in_specs=[
            pl.BlockSpec(memory_space=pltpu.SMEM),
            pl.BlockSpec(memory_space=pltpu.SMEM),
            pl.BlockSpec(
                (None, None, kinds, None, parts, slab, rows, lanes),
                lambda m, c: (0, begin + m, 0, c, 0, 0, 0, 0),
            ),
        ]
        + [pl.BlockSpec(memory_space=pltpu.VMEM)] * len(before)
        + [pl.BlockSpec(memory_space=pl.ANY)] * len(after),
        out_specs=[
            pl.BlockSpec(whole, lambda m, c: (0, 0, 0)),
            pl.BlockSpec((8, lanes), lambda m, c: (0, 0)),
        ]
        + [pl.BlockSpec((None, None) + edges[2:], lambda m, c: (m, c, 0, 0, 0, 0))] * 2,
        out_shape=[
            pltpu.VMEM(whole, jnp.float32),
            jax.ShapeDtypeStruct((8, lanes), jnp.float32),
            pltpu.HBM(edges, jnp.float32),
            pltpu.VMEM(edges, jnp.float32),
        ],
        scratch_shapes=[
            pltpu.VMEM((fields, slab + 2, rows + 2 * MARGIN, lanes), jnp.float32),
            pltpu.VMEM((fields, slab, rows, lanes), jnp.float32),
        ],
        compiler_params=pltpu.CompilerParams(vmem_limit_bytes=INTERIOR_VMEM),
        cost_estimate=pl.CostEstimate(flops=INTERIOR_FLOPS, bytes_accessed=1024, transcendentals=0),
    )(sides, weights, saved_modes, *before, *after)


def strain_of(ref, mode):
    return lambda half, kind, part, start: ref[mode, half, kind, part, pl.ds(start, STEP)]


def halo_of(ref, mode):
    return lambda half, kind, part, start: ref[mode, kind, half, part, pl.ds(start, STEP)]


def outer_plane(start, shape, scales, strains, halos):
    halves, parts = shape
    total = None
    for scale, strain, halo in zip(scales, strains, halos, strict=True):
        found = None
        for half in range(halves):
            for part in range(parts):
                u, v = (
                    strain(half, kind, part, start) + halo(half, kind, part, start).astype(jnp.float32)
                    for kind in range(2)
                )
                term = u * v
                if part == 0:
                    term = 2.0 * term
                found = term if found is None else found + term
        found = scale * found
        total = found if total is None else total + found
    return total


def far_kernel(groups, side_ref, weight_ref, edge_ref, *refs):
    halo_refs = refs[:-3]
    sens_ref, turns_ref, tall_ref = refs[-3:]
    scales, strains, halos = [], [], []
    for (begin, count), halo_ref in zip(groups, halo_refs, strict=True):
        for mode in range(begin, begin + count):
            scales.append(weight_ref[0, mode])
            strains.append(strain_of(edge_ref, mode))
            halos.append(halo_of(halo_ref, mode - begin))
    slab = sens_ref.shape[0]
    _, halves, _, parts, rows, _ = edge_ref.shape
    count, _, tall, _ = turns_ref.shape
    band = tall - 2 * EDGE
    far = side_ref[0] * (slab - 1)
    tall_ref[...] = sens_ref[far]
    for start in range(0, rows, STEP):
        tall_ref[pl.ds(MARGIN + start, STEP)] += outer_plane(start, (halves, parts), scales, strains, halos)
    for piece in range(count):
        index, bits = 0, 1
        while bits < count:
            index = 2 * index + (piece // bits) % 2
            bits *= 2
        start = index * band + MARGIN - EDGE
        turns_ref[piece] = sens_ref[:, pl.ds(start, tall)]
        turns_ref[piece, far] = tall_ref[pl.ds(start, tall)]


def finish_far(sides, weights, groups, edges, halos, sens, freqs):
    slab, rows, lanes = sens.shape
    band = (rows - 2 * MARGIN) // freqs
    return pl.pallas_call(
        functools.partial(far_kernel, groups),
        in_specs=[pl.BlockSpec(memory_space=pltpu.SMEM)] * 2
        + [pl.BlockSpec(memory_space=pltpu.VMEM)] * (len(halos) + 2),
        out_specs=pl.BlockSpec(memory_space=pltpu.VMEM),
        out_shape=jax.ShapeDtypeStruct((freqs, slab, band + 2 * EDGE, lanes), jnp.float32),
        scratch_shapes=[pltpu.VMEM((rows, lanes), jnp.float32)],
        compiler_params=pltpu.CompilerParams(vmem_limit_bytes=SMALL_VMEM),
        cost_estimate=QUICK,
    )(sides, weights, edges, *halos, sens)


def fetch_kernel(count, *refs):
    sources, outs, sems = refs[:count], refs[-1 - count : -1], refs[-1]
    copies = [pltpu.make_async_copy(sources[i], outs[i], sems.at[i]) for i in range(count)]
    for copy in copies:
        copy.start()
    for copy in copies:
        copy.wait()


def fetch(blocks, after):
    return pl.pallas_call(
        functools.partial(fetch_kernel, len(blocks)),
        in_specs=[pl.BlockSpec(memory_space=pl.ANY)] * (len(blocks) + len(after)),
        out_specs=[pl.BlockSpec(memory_space=pltpu.VMEM)] * len(blocks),
        out_shape=[pltpu.VMEM(block.shape, block.dtype) for block in blocks],
        scratch_shapes=[pltpu.SemaphoreType.DMA((len(blocks),))],
        compiler_params=pltpu.CompilerParams(vmem_limit_bytes=SMALL_VMEM),
        cost_estimate=QUICK,
    )(*[hbm(block) for block in blocks], *after)


def near_kernel(count, side_ref, weight_ref, edge_ref, *refs):
    halo_refs, (keep_ref, give_ref, tall_ref) = refs[:count], refs[count:]
    modes, halves, _, parts, rows, _ = edge_ref.shape
    scales = [weight_ref[0, mode] for mode in range(modes)]
    strains = [strain_of(edge_ref, mode) for mode in range(modes)]
    halos = [halo_of(ref, mode) for ref in halo_refs for mode in range(ref.shape[0])]
    _, tall, lanes = keep_ref.shape
    band = tall - 2 * EDGE
    empty = jnp.zeros((2 * EDGE, lanes), jnp.float32)
    tall_ref[pl.ds(0, 2 * EDGE)] = empty
    tall_ref[pl.ds(rows, 2 * EDGE)] = empty
    for start in range(0, rows, STEP):
        tall_ref[pl.ds(EDGE + start, STEP)] = outer_plane(start, (halves, parts), scales, strains, halos)
    for turn, ref in enumerate((keep_ref, give_ref, keep_ref, give_ref)):
        start = pl.multiple_of((side_ref[1] ^ turn) * band, 8)
        ref[turn // 2] = tall_ref[pl.ds(start, tall)]


def finish_near(sides, weights, edges, halos, freqs):
    rows, lanes = edges.shape[4:]
    bands = jax.ShapeDtypeStruct((2, rows // freqs + 2 * EDGE, lanes), jnp.float32)
    return pl.pallas_call(
        functools.partial(near_kernel, len(halos)),
        in_specs=[pl.BlockSpec(memory_space=pltpu.SMEM)] * 2
        + [pl.BlockSpec(memory_space=pltpu.VMEM)] * (1 + len(halos)),
        out_specs=[pl.BlockSpec(memory_space=pltpu.VMEM)] * 2,
        out_shape=[bands] * 2,
        scratch_shapes=[pltpu.VMEM((rows + 2 * EDGE, lanes), jnp.float32)],
        compiler_params=pltpu.CompilerParams(vmem_limit_bytes=SMALL_VMEM),
        cost_estimate=QUICK,
    )(sides, weights, edges, *halos)


def pair_kernel(keep_ref, found_ref, own_ref, other_ref):
    own_ref[...] = keep_ref[0] + found_ref[0]
    other_ref[...] = keep_ref[1] + found_ref[1]


def pair_sum(keep, found):
    band = jax.ShapeDtypeStruct(keep.shape[1:], jnp.float32)
    return pl.pallas_call(
        pair_kernel,
        in_specs=[pl.BlockSpec(memory_space=pltpu.VMEM)] * 2,
        out_specs=[pl.BlockSpec(memory_space=pltpu.VMEM)] * 2,
        out_shape=[band] * 2,
        compiler_params=pltpu.CompilerParams(vmem_limit_bytes=SMALL_VMEM),
        cost_estimate=QUICK,
    )(keep, found)


class Pass:
    def __init__(self, tall, lanes, first_y, total_y):
        self.tall, self.lanes = tall, lanes
        self.lane = lax.broadcasted_iota(jnp.int32, (tall, lanes), 1)
        row = lax.broadcasted_iota(jnp.int32, (tall, lanes), 0) + (first_y - EDGE)
        self.inside = (row >= 0) & (row < total_y)

    def __call__(self, below, center, above):
        axial = above + below - 2.0 * center
        cross = (
            pltpu.roll(center, self.tall - 1, 0)
            + pltpu.roll(center, 1, 0)
            + jnp.where(self.lane == self.lanes - 1, 0.0, pltpu.roll(center, self.lanes - 1, 1))
            + jnp.where(self.lane == 0, 0.0, pltpu.roll(center, 1, 1))
            - 4.0 * center
        )
        return jnp.where(self.inside, center + AXIAL * axial + CROSS * cross, 0.0)


def smooth_kernel(total_x, total_y, place_ref, base_ref, near_ref, far_ref, out_ref, one_ref, two_ref):
    slab, tall, lanes = base_ref.shape
    first_x = place_ref[1]
    even = place_ref[0] == 0
    one_ref[pl.ds(3, slab)] = base_ref[...]
    near = near_ref[...]
    far = far_ref[...]
    one_ref[pl.ds(0, 3)] = jnp.where(even, far, near)
    one_ref[pl.ds(slab + 3, 3)] = jnp.where(even, near, far)
    smoothed = Pass(tall, lanes, place_ref[2], total_y)

    def clear(ref, plane):
        x = first_x + (plane - 3)

        @pl.when((x < 0) | (x >= total_x))
        def _():
            ref[plane] = jnp.zeros_like(ref[plane])

    def passed(source, plane):
        return smoothed(source[plane - 1], source[plane], source[plane + 1])

    for plane in range(1, slab + 5):
        two_ref[plane] = passed(one_ref, plane)
    for plane in (1, 2, slab + 3, slab + 4):
        clear(two_ref, plane)
    for plane in range(2, slab + 4):
        one_ref[plane] = passed(two_ref, plane)
    for plane in (2, slab + 3):
        clear(one_ref, plane)
    for plane in range(3, slab + 3):
        out_ref[plane - 3] = passed(one_ref, plane)[EDGE : tall - EDGE]


def smooth(place, base, near, far, total_x, total_y):
    slab, tall, lanes = base.shape
    return pl.pallas_call(
        functools.partial(smooth_kernel, total_x, total_y),
        in_specs=[pl.BlockSpec(memory_space=pltpu.SMEM)]
        + [pl.BlockSpec(memory_space=pltpu.VMEM)] * 3,
        out_specs=pl.BlockSpec(memory_space=pltpu.VMEM),
        out_shape=pltpu.VMEM((slab, tall - 2 * EDGE, lanes), jnp.float32),
        scratch_shapes=[pltpu.VMEM((slab + 6, tall, lanes), jnp.float32)] * 2,
        compiler_params=pltpu.CompilerParams(vmem_limit_bytes=SMALL_VMEM),
        cost_estimate=pl.CostEstimate(flops=SMOOTH_FLOPS, bytes_accessed=1024, transcendentals=0),
    )(place, base, near, far)


def add_near_kernel(total_y, place_ref, own_refs, beyond_refs, before_ref, out_ref):
    tall, lanes = own_refs[0].shape
    slab = before_ref.shape[0]
    even = place_ref[0] == 0
    first = jnp.where(even, slab - 4, 0)
    out_ref[...] = before_ref[...]
    smoothed = Pass(tall, lanes, place_ref[2], total_y)
    own, beyond = (refs[0][...] + refs[1][...] for refs in (own_refs, beyond_refs))
    zero = jnp.zeros_like(own)
    planes = {-1: beyond, 0: own}
    for reach in (1, 2, 3):
        low, high = max(-1 - reach, reach - 4), min(reach, 3)
        planes = {
            at: smoothed(planes.get(at - 1, zero), planes.get(at, zero), planes.get(at + 1, zero))
            for at in range(low, high + 1)
        }
    for at in range(4):
        out_ref[first + jnp.where(even, 3 - at, at)] += planes[at][EDGE : tall - EDGE]


def add_near(place, own, beyond, before, total_y):
    slab, band, lanes = before.shape
    return pl.pallas_call(
        functools.partial(add_near_kernel, total_y),
        in_specs=[pl.BlockSpec(memory_space=pltpu.SMEM)]
        + [[pl.BlockSpec(memory_space=pltpu.VMEM)] * 2] * 2
        + [pl.BlockSpec(memory_space=pltpu.VMEM)],
        out_specs=pl.BlockSpec(memory_space=pltpu.VMEM),
        out_shape=jax.ShapeDtypeStruct(before.shape, jnp.float32),
        compiler_params=pltpu.CompilerParams(vmem_limit_bytes=SMALL_VMEM),
        cost_estimate=QUICK,
    )(place, own, beyond, before)


def swap(block, axis, pairs):
    return lax.ppermute(block, axis, [p for a, b in pairs for p in ((a, b), (b, a))])


def both(freq_pairs, space_pairs, slabs):
    return [(f * slabs + s, g * slabs + r) for f, g in freq_pairs for s, r in space_pairs]


def near_sums(keep, give, near_pairs):
    freqs, slabs = lax.axis_size("freq"), lax.axis_size("space")
    own, other = pair_sum(keep, lax.ppermute(give, "freq", [(i, i ^ 1) for i in range(freqs)]))
    across = [(i, i ^ 2) for i in range(freqs)]
    swaps = [p for a, b in near_pairs for p in ((a, b), (b, a))]
    from_own = lax.ppermute(other, "freq", across)
    beyond = lax.ppermute(own, "space", swaps)
    from_beyond = lax.ppermute(other, ("freq", "space"), both(across, swaps, slabs))
    return [own, from_own], [beyond, from_beyond]


def hbm(block):
    return pltpu.with_memory_space_constraint(block, pltpu.HBM)


def split_kernel(side_ref, found_ref, send_ref, keep_ref):
    half = keep_ref.shape[0]
    which = side_ref[1] // 2 % 2
    for ref, side in ((keep_ref, which), (send_ref, 1 - which)):
        for piece in range(half):
            at = side * half + piece
            ref[piece] = found_ref[at] + found_ref[2 * half + at]


def split(sides, found):
    shape = (found.shape[0] // 4,) + found.shape[1:]
    return pl.pallas_call(
        split_kernel,
        in_specs=[pl.BlockSpec(memory_space=pltpu.SMEM), pl.BlockSpec(memory_space=pltpu.VMEM)],
        out_specs=[pl.BlockSpec(memory_space=pltpu.VMEM)] * 2,
        out_shape=[pltpu.VMEM(shape, jnp.float32)] * 2,
        compiler_params=pltpu.CompilerParams(vmem_limit_bytes=SMALL_VMEM),
        cost_estimate=QUICK,
    )(sides, found)


def base_kernel(side_ref, keep_ref, found_ref, *refs):
    base_ref, near_ref, far_ref = refs[-3:]
    slab, depth = base_ref.shape[0], near_ref.shape[0]
    base_ref[...] = keep_ref[0] + found_ref[0]
    start = (1 - side_ref[0]) * (slab - depth)
    near_ref[...] = base_ref[pl.ds(start, depth)]
    far_ref[...] = base_ref[pl.ds(slab - depth - start, depth)]


def finish_base(sides, keep, found, after):
    _, slab, tall, lanes = keep.shape
    return pl.pallas_call(
        base_kernel,
        in_specs=[pl.BlockSpec(memory_space=pltpu.SMEM)]
        + [pl.BlockSpec(memory_space=pltpu.VMEM)] * 2
        + [pl.BlockSpec(memory_space=pl.ANY)] * len(after),
        out_specs=[pl.BlockSpec(memory_space=pltpu.VMEM)] * 3,
        out_shape=[pltpu.VMEM((count, tall, lanes), jnp.float32) for count in (slab, 3, 3)],
        compiler_params=pltpu.CompilerParams(vmem_limit_bytes=SMALL_VMEM),
        cost_estimate=QUICK,
    )(sides, keep, found, *after)


def band_sum(sides, turns):
    count = lax.axis_size("freq")
    groups = [[i, i + 1] for i in range(0, count, 2)]
    send, keep = split(sides, lax.all_to_all(turns, "freq", 0, 0, axis_index_groups=groups, tiled=True))
    found = lax.ppermute(send, "freq", [(i, i ^ 2) for i in range(count)])
    return *finish_base(sides, keep, found, []), keep


def local(saved_modes, mode_gains):
    _, modes, kinds, halves, parts, slab, rows, lanes = saved_modes.shape
    freqs = lax.axis_size("freq")
    slabs = lax.axis_size("space")
    factor = -2.0 / (saved_modes.shape[0] * freqs * modes)
    weights = (factor / 8.0) * mode_gains
    place = lax.axis_index("space")
    odd = place % 2
    near_pairs = [(i, i + 1) for i in range(0, slabs - 1, 2)]
    far_pairs = [(i, i + 1) for i in range(1, slabs - 1, 2)]

    def outer(plane, begin, count):
        start = (0, begin, 0, 0, 0, plane, 0, 0)
        found = lax.dynamic_slice(saved_modes, start, (1, count, kinds, halves, parts, 1, rows, lanes))
        return found.reshape((count, kinds, halves, parts, rows, lanes))

    near_plane = jnp.where(odd == 0, slab - 1, 0)
    half = modes // 2
    groups = [(0, half), (half, modes - half)]
    (first_out,) = planes(saved_modes, near_plane, [(0, 1)], [])
    (near_out,) = planes(saved_modes, near_plane, [(1, modes - 1)], [first_out])
    near_halos = [swap(block, "space", near_pairs) for block in (first_out, near_out)]
    far_outs = planes(saved_modes, slab - 1 - near_plane, groups, [near_out])
    far_halos = [swap(block, "space", far_pairs) for block in far_outs]

    sides = jnp.stack([odd, lax.axis_index("freq")]).astype(jnp.int32)
    sens, _, near_edges, far_edges = interior(saved_modes, weights, sides, 0, modes, [], far_outs)
    turns = finish_far(sides, weights, groups, far_edges, far_halos, sens, freqs)
    base, near, far, keep = band_sum(sides, turns)
    near, far = swap(near, "space", near_pairs), swap(far, "space", far_pairs)
    where = jnp.stack([odd, place * slab, lax.axis_index("freq") * (rows // freqs)]).astype(jnp.int32)
    smoothed = smooth(where, base, near, far, slab * slabs, rows)

    keep, give = finish_near(sides, weights, *fetch([near_edges], [keep]), near_halos, freqs)
    return add_near(where, *near_sums(keep, give, near_pairs), smoothed, rows)


def solution(mesh):
    in_specs = (P("freq", None, None, None, None, "space", None, None), P("freq", None))
    out_specs = P("space", "freq", None)
    return jax.shard_map(local, mesh=mesh, in_specs=in_specs, out_specs=out_specs, check_vma=False)
```

```python
import functools

import jax
import jax.numpy as jnp
from jax import lax
from jax.experimental import pallas as pl
from jax.experimental.pallas import tpu as pltpu
from jax.sharding import PartitionSpec as P

AXIAL = 0.35
CROSS = 0.06
MARGIN = 8
EDGE = 4
STEP = 16
INTERIOR_VMEM = 30 * 1024 * 1024
QUICK = pl.CostEstimate(flops=1024, bytes_accessed=1024, transcendentals=0)
INTERIOR_FLOPS = 8 * 10**9
SMOOTH_FLOPS = 10**10
SMALL_VMEM = 16 * 1024 * 1024


def plane_kernel(begin, plane_ref, modes_ref, *refs):
    out_refs, sems = refs[-1 - len(begin) : -1], refs[-1]
    copies = []
    for at, (first, out_ref) in enumerate(zip(begin, out_refs, strict=True)):
        source = modes_ref.at[0, pl.ds(first, out_ref.shape[0]), :, :, :, plane_ref[0]]
        copies.append(pltpu.make_async_copy(source, out_ref, sems.at[at]))
        copies[-1].start()
    for copy in copies:
        copy.wait()


def planes(saved_modes, plane, groups, after):
    _, _, kinds, halves, parts, _, rows, lanes = saved_modes.shape
    return pl.pallas_call(
        functools.partial(plane_kernel, [first for first, _ in groups]),
        in_specs=[pl.BlockSpec(memory_space=pltpu.SMEM), pl.BlockSpec(memory_space=pl.ANY)]
        + [pl.BlockSpec(memory_space=pl.ANY)] * len(after),
        out_specs=[pl.BlockSpec(memory_space=pltpu.VMEM)] * len(groups),
        out_shape=[
            pltpu.VMEM((count, kinds, halves, parts, rows, lanes), saved_modes.dtype) for _, count in groups
        ],
        scratch_shapes=[pltpu.SemaphoreType.DMA((len(groups),))],
        compiler_params=pltpu.CompilerParams(vmem_limit_bytes=SMALL_VMEM),
        cost_estimate=QUICK,
    )(plane.reshape(1).astype(jnp.int32), hbm(saved_modes), *after)


def interior_kernel(begin, before, after, side_ref, weight_ref, modes_ref, *refs):
    sens_ref, token_ref, near_edge_ref, far_edge_ref, wide_ref, lane_ref = refs[before + after :]
    slab, rows, lanes = modes_ref.shape[2:]

    @pl.when((pl.program_id(0) == 0) & (pl.program_id(1) == 0))
    def _():
        sens_ref[...] = refs[0][...] if before else jnp.zeros_like(sens_ref)
        token_ref[...] = jnp.zeros_like(token_ref)
        for plane in (0, slab + 1):
            wide_ref[:, plane] = jnp.zeros_like(wide_ref[:, plane])
        for start in (0, MARGIN + rows):
            wide_ref[:, :, pl.ds(start, MARGIN)] = jnp.zeros_like(wide_ref[:, :, pl.ds(start, MARGIN)])

    source = lax.broadcasted_iota(jnp.int32, (lanes, lanes), 0)
    target = lax.broadcasted_iota(jnp.int32, (lanes, lanes), 1)
    difference = jnp.where(source == target + 1, 1.0, 0.0) - jnp.where(source == target - 1, 1.0, 0.0)
    difference = difference.astype(jnp.bfloat16)
    lane = lax.broadcasted_iota(jnp.int32, (STEP, lanes), 1)
    not_last = jnp.where(lane == lanes - 1, 0.0, 1.0)
    not_first = jnp.where(lane == 0, 0.0, 1.0)
    scale = weight_ref[0, begin + pl.program_id(0)]

    def load_plane(plane):
        for kind in range(2):
            for part in range(3):
                values = modes_ref[kind, part, plane]
                field = kind * 3 + part
                wide_ref[field, plane + 1, MARGIN : MARGIN + rows] = values.astype(jnp.float32)
                if part > 0:
                    lane_ref[field, plane] = jnp.dot(
                        values, difference, preferred_element_type=jnp.float32
                    )

    def terms(plane, start):
        sides = []
        for kind in range(2):

            def axial(part):
                field = kind * 3 + part
                return (
                    wide_ref[field, plane + 2, pl.ds(MARGIN + start, STEP)]
                    - wide_ref[field, plane, pl.ds(MARGIN + start, STEP)]
                )

            def by_row(part):
                field = kind * 3 + part
                return (
                    wide_ref[field, plane + 1, pl.ds(MARGIN + start + 1, STEP)]
                    - wide_ref[field, plane + 1, pl.ds(MARGIN + start - 1, STEP)]
                )

            def by_lane(part):
                if part > 0:
                    return lane_ref[kind * 3 + part, plane, pl.ds(start, STEP)]
                values = modes_ref[kind, part, plane, pl.ds(start, STEP)]
                upper = pltpu.roll(values, lanes - 1, 1).astype(jnp.float32)
                lower = pltpu.roll(values, 1, 1).astype(jnp.float32)
                return upper * not_last - lower * not_first

            outer = (axial(0), axial(1) + by_row(0), axial(2) + by_lane(0))
            inner = (by_row(1), by_lane(2), by_row(2) + by_lane(1))
            sides.append((outer, inner))
        return sides

    def inner_plane(plane):
        for start in range(0, rows, STEP):
            (ou, iu), (ov, iv) = terms(plane, start)
            diagonal = ou[0] * ov[0] + iu[0] * iv[0] + iu[1] * iv[1]
            mixed = ou[1] * ov[1] + ou[2] * ov[2] + iu[2] * iv[2]
            sens_ref[plane, pl.ds(MARGIN + start, STEP)] += scale * (2.0 * diagonal + mixed)

    def both(plane, carry):
        load_plane(plane + 1)
        inner_plane(plane)
        return carry

    load_plane(0)
    load_plane(1)
    lax.fori_loop(1, slab - 1, both, 0, unroll=True)

    odd = side_ref[0]
    near = (1 - odd) * (slab - 1)
    for edge_ref, plane, sign in (
        (near_edge_ref, near, 1.0 - 2.0 * odd.astype(jnp.float32)),
        (far_edge_ref, slab - 1 - near, 2.0 * odd.astype(jnp.float32) - 1.0),
    ):
        for start in range(0, rows, STEP):
            (ou, iu), (ov, iv) = terms(plane, start)
            diagonal = iu[0] * iv[0] + iu[1] * iv[1]
            mixed = iu[2] * iv[2]
            sens_ref[plane, pl.ds(MARGIN + start, STEP)] += scale * (2.0 * diagonal + mixed)
            for part in range(3):
                edge_ref[0, part, pl.ds(start, STEP)] = sign * ou[part]
                edge_ref[1, part, pl.ds(start, STEP)] = sign * ov[part]


def interior(saved_modes, weights, sides, begin, count, before, after):
    _, _, kinds, halves, parts, slab, rows, lanes = saved_modes.shape
    whole = (slab, rows + 2 * MARGIN, lanes)
    edges = (count, halves, kinds, parts, rows, lanes)
    fields = kinds * parts
    return pl.pallas_call(
        functools.partial(interior_kernel, begin, len(before), len(after)),
        grid=(count, halves),
        in_specs=[
            pl.BlockSpec(memory_space=pltpu.SMEM),
            pl.BlockSpec(memory_space=pltpu.SMEM),
            pl.BlockSpec(
                (None, None, kinds, None, parts, slab, rows, lanes),
                lambda m, c: (0, begin + m, 0, c, 0, 0, 0, 0),
            ),
        ]
        + [pl.BlockSpec(memory_space=pltpu.VMEM)] * len(before)
        + [pl.BlockSpec(memory_space=pl.ANY)] * len(after),
        out_specs=[
            pl.BlockSpec(whole, lambda m, c: (0, 0, 0)),
            pl.BlockSpec((8, lanes), lambda m, c: (0, 0)),
        ]
        + [pl.BlockSpec((None, None) + edges[2:], lambda m, c: (m, c, 0, 0, 0, 0))] * 2,
        out_shape=[
            pltpu.VMEM(whole, jnp.float32),
            jax.ShapeDtypeStruct((8, lanes), jnp.float32),
            pltpu.HBM(edges, jnp.float32),
            pltpu.VMEM(edges, jnp.float32),
        ],
        scratch_shapes=[
            pltpu.VMEM((fields, slab + 2, rows + 2 * MARGIN, lanes), jnp.float32),
            pltpu.VMEM((fields, slab, rows, lanes), jnp.float32),
        ],
        compiler_params=pltpu.CompilerParams(vmem_limit_bytes=INTERIOR_VMEM),
        cost_estimate=pl.CostEstimate(flops=INTERIOR_FLOPS, bytes_accessed=1024, transcendentals=0),
    )(sides, weights, saved_modes, *before, *after)


def strain_of(ref, mode):
    return lambda half, kind, part, start: ref[mode, half, kind, part, pl.ds(start, STEP)]


def halo_of(ref, mode):
    return lambda half, kind, part, start: ref[mode, kind, half, part, pl.ds(start, STEP)]


def outer_plane(start, shape, scales, strains, halos):
    halves, parts = shape
    total = None
    for scale, strain, halo in zip(scales, strains, halos, strict=True):
        found = None
        for half in range(halves):
            for part in range(parts):
                u, v = (
                    strain(half, kind, part, start) + halo(half, kind, part, start).astype(jnp.float32)
                    for kind in range(2)
                )
                term = u * v
                if part == 0:
                    term = 2.0 * term
                found = term if found is None else found + term
        found = scale * found
        total = found if total is None else total + found
    return total


def far_kernel(groups, side_ref, weight_ref, edge_ref, *refs):
    halo_refs = refs[:-3]
    sens_ref, turns_ref, tall_ref = refs[-3:]
    scales, strains, halos = [], [], []
    for (begin, count), halo_ref in zip(groups, halo_refs, strict=True):
        for mode in range(begin, begin + count):
            scales.append(weight_ref[0, mode])
            strains.append(strain_of(edge_ref, mode))
            halos.append(halo_of(halo_ref, mode - begin))
    slab = sens_ref.shape[0]
    _, halves, _, parts, rows, _ = edge_ref.shape
    count, _, tall, _ = turns_ref.shape
    band = tall - 2 * EDGE
    far = side_ref[0] * (slab - 1)
    tall_ref[...] = sens_ref[far]
    for start in range(0, rows, STEP):
        tall_ref[pl.ds(MARGIN + start, STEP)] += outer_plane(start, (halves, parts), scales, strains, halos)
    for piece in range(count):
        index, bits = 0, 1
        while bits < count:
            index = 2 * index + (piece // bits) % 2
            bits *= 2
        start = index * band + MARGIN - EDGE
        turns_ref[piece] = sens_ref[:, pl.ds(start, tall)]
        turns_ref[piece, far] = tall_ref[pl.ds(start, tall)]


def finish_far(sides, weights, groups, edges, halos, sens, freqs):
    slab, rows, lanes = sens.shape
    band = (rows - 2 * MARGIN) // freqs
    return pl.pallas_call(
        functools.partial(far_kernel, groups),
        in_specs=[pl.BlockSpec(memory_space=pltpu.SMEM)] * 2
        + [pl.BlockSpec(memory_space=pltpu.VMEM)] * (len(halos) + 2),
        out_specs=pl.BlockSpec(memory_space=pltpu.VMEM),
        out_shape=jax.ShapeDtypeStruct((freqs, slab, band + 2 * EDGE, lanes), jnp.float32),
        scratch_shapes=[pltpu.VMEM((rows, lanes), jnp.float32)],
        compiler_params=pltpu.CompilerParams(vmem_limit_bytes=SMALL_VMEM),
        cost_estimate=QUICK,
    )(sides, weights, edges, *halos, sens)


def fetch_kernel(count, *refs):
    sources, outs, sems = refs[:count], refs[-1 - count : -1], refs[-1]
    copies = [pltpu.make_async_copy(sources[i], outs[i], sems.at[i]) for i in range(count)]
    for copy in copies:
        copy.start()
    for copy in copies:
        copy.wait()


def fetch(blocks, after):
    return pl.pallas_call(
        functools.partial(fetch_kernel, len(blocks)),
        in_specs=[pl.BlockSpec(memory_space=pl.ANY)] * (len(blocks) + len(after)),
        out_specs=[pl.BlockSpec(memory_space=pltpu.VMEM)] * len(blocks),
        out_shape=[pltpu.VMEM(block.shape, block.dtype) for block in blocks],
        scratch_shapes=[pltpu.SemaphoreType.DMA((len(blocks),))],
        compiler_params=pltpu.CompilerParams(vmem_limit_bytes=SMALL_VMEM),
        cost_estimate=QUICK,
    )(*[hbm(block) for block in blocks], *after)


def near_kernel(count, side_ref, weight_ref, edge_ref, *refs):
    halo_refs, (keep_ref, give_ref, tall_ref) = refs[:count], refs[count:]
    modes, halves, _, parts, rows, _ = edge_ref.shape
    scales = [weight_ref[0, mode] for mode in range(modes)]
    strains = [strain_of(edge_ref, mode) for mode in range(modes)]
    halos = [halo_of(ref, mode) for ref in halo_refs for mode in range(ref.shape[0])]
    _, tall, lanes = keep_ref.shape
    band = tall - 2 * EDGE
    empty = jnp.zeros((2 * EDGE, lanes), jnp.float32)
    tall_ref[pl.ds(0, 2 * EDGE)] = empty
    tall_ref[pl.ds(rows, 2 * EDGE)] = empty
    for start in range(0, rows, STEP):
        tall_ref[pl.ds(EDGE + start, STEP)] = outer_plane(start, (halves, parts), scales, strains, halos)
    for turn, ref in enumerate((keep_ref, give_ref, keep_ref, give_ref)):
        start = pl.multiple_of((side_ref[1] ^ turn) * band, 8)
        ref[turn // 2] = tall_ref[pl.ds(start, tall)]


def finish_near(sides, weights, edges, halos, freqs):
    rows, lanes = edges.shape[4:]
    bands = jax.ShapeDtypeStruct((2, rows // freqs + 2 * EDGE, lanes), jnp.float32)
    return pl.pallas_call(
        functools.partial(near_kernel, len(halos)),
        in_specs=[pl.BlockSpec(memory_space=pltpu.SMEM)] * 2
        + [pl.BlockSpec(memory_space=pltpu.VMEM)] * (1 + len(halos)),
        out_specs=[pl.BlockSpec(memory_space=pltpu.VMEM)] * 2,
        out_shape=[bands] * 2,
        scratch_shapes=[pltpu.VMEM((rows + 2 * EDGE, lanes), jnp.float32)],
        compiler_params=pltpu.CompilerParams(vmem_limit_bytes=SMALL_VMEM),
        cost_estimate=QUICK,
    )(sides, weights, edges, *halos)


def pair_kernel(keep_ref, found_ref, own_ref, other_ref):
    own_ref[...] = keep_ref[0] + found_ref[0]
    other_ref[...] = keep_ref[1] + found_ref[1]


def pair_sum(keep, found):
    band = jax.ShapeDtypeStruct(keep.shape[1:], jnp.float32)
    return pl.pallas_call(
        pair_kernel,
        in_specs=[pl.BlockSpec(memory_space=pltpu.VMEM)] * 2,
        out_specs=[pl.BlockSpec(memory_space=pltpu.VMEM)] * 2,
        out_shape=[band] * 2,
        compiler_params=pltpu.CompilerParams(vmem_limit_bytes=SMALL_VMEM),
        cost_estimate=QUICK,
    )(keep, found)


class Pass:
    def __init__(self, tall, lanes, first_y, total_y):
        self.tall, self.lanes = tall, lanes
        self.lane = lax.broadcasted_iota(jnp.int32, (tall, lanes), 1)
        row = lax.broadcasted_iota(jnp.int32, (tall, lanes), 0) + (first_y - EDGE)
        self.inside = (row >= 0) & (row < total_y)

    def __call__(self, below, center, above):
        axial = above + below - 2.0 * center
        cross = (
            pltpu.roll(center, self.tall - 1, 0)
            + pltpu.roll(center, 1, 0)
            + jnp.where(self.lane == self.lanes - 1, 0.0, pltpu.roll(center, self.lanes - 1, 1))
            + jnp.where(self.lane == 0, 0.0, pltpu.roll(center, 1, 1))
            - 4.0 * center
        )
        return jnp.where(self.inside, center + AXIAL * axial + CROSS * cross, 0.0)


def smooth_kernel(total_x, total_y, place_ref, base_ref, near_ref, far_ref, out_ref, one_ref, two_ref):
    slab, tall, lanes = base_ref.shape
    first_x = place_ref[1]
    even = place_ref[0] == 0
    one_ref[pl.ds(3, slab)] = base_ref[...]
    near = near_ref[...]
    far = far_ref[...]
    one_ref[pl.ds(0, 3)] = jnp.where(even, far, near)
    one_ref[pl.ds(slab + 3, 3)] = jnp.where(even, near, far)
    smoothed = Pass(tall, lanes, place_ref[2], total_y)

    def clear(ref, plane):
        x = first_x + (plane - 3)

        @pl.when((x < 0) | (x >= total_x))
        def _():
            ref[plane] = jnp.zeros_like(ref[plane])

    def passed(source, plane):
        return smoothed(source[plane - 1], source[plane], source[plane + 1])

    for plane in range(1, slab + 5):
        two_ref[plane] = passed(one_ref, plane)
    for plane in (1, 2, slab + 3, slab + 4):
        clear(two_ref, plane)
    for plane in range(2, slab + 4):
        one_ref[plane] = passed(two_ref, plane)
    for plane in (2, slab + 3):
        clear(one_ref, plane)
    for plane in range(3, slab + 3):
        out_ref[plane - 3] = passed(one_ref, plane)[EDGE : tall - EDGE]


def smooth(place, base, near, far, total_x, total_y):
    slab, tall, lanes = base.shape
    return pl.pallas_call(
        functools.partial(smooth_kernel, total_x, total_y),
        in_specs=[pl.BlockSpec(memory_space=pltpu.SMEM)]
        + [pl.BlockSpec(memory_space=pltpu.VMEM)] * 3,
        out_specs=pl.BlockSpec(memory_space=pltpu.VMEM),
        out_shape=pltpu.VMEM((slab, tall - 2 * EDGE, lanes), jnp.float32),
        scratch_shapes=[pltpu.VMEM((slab + 6, tall, lanes), jnp.float32)] * 2,
        compiler_params=pltpu.CompilerParams(vmem_limit_bytes=SMALL_VMEM),
        cost_estimate=pl.CostEstimate(flops=SMOOTH_FLOPS, bytes_accessed=1024, transcendentals=0),
    )(place, base, near, far)


def add_near_kernel(total_y, place_ref, own_refs, beyond_refs, before_ref, out_ref):
    tall, lanes = own_refs[0].shape
    slab = before_ref.shape[0]
    even = place_ref[0] == 0
    first = jnp.where(even, slab - 4, 0)
    out_ref[...] = before_ref[...]
    smoothed = Pass(tall, lanes, place_ref[2], total_y)
    own, beyond = (refs[0][...] + refs[1][...] for refs in (own_refs, beyond_refs))
    zero = jnp.zeros_like(own)
    planes = {-1: beyond, 0: own}
    for reach in (1, 2, 3):
        low, high = max(-1 - reach, reach - 4), min(reach, 3)
        planes = {
            at: smoothed(planes.get(at - 1, zero), planes.get(at, zero), planes.get(at + 1, zero))
            for at in range(low, high + 1)
        }
    for at in range(4):
        out_ref[first + jnp.where(even, 3 - at, at)] += planes[at][EDGE : tall - EDGE]


def add_near(place, own, beyond, before, total_y):
    slab, band, lanes = before.shape
    return pl.pallas_call(
        functools.partial(add_near_kernel, total_y),
        in_specs=[pl.BlockSpec(memory_space=pltpu.SMEM)]
        + [[pl.BlockSpec(memory_space=pltpu.VMEM)] * 2] * 2
        + [pl.BlockSpec(memory_space=pltpu.VMEM)],
        out_specs=pl.BlockSpec(memory_space=pltpu.VMEM),
        out_shape=jax.ShapeDtypeStruct(before.shape, jnp.float32),
        compiler_params=pltpu.CompilerParams(vmem_limit_bytes=SMALL_VMEM),
        cost_estimate=QUICK,
    )(place, own, beyond, before)


def swap(block, axis, pairs):
    return lax.ppermute(block, axis, [p for a, b in pairs for p in ((a, b), (b, a))])


def both(freq_pairs, space_pairs, slabs):
    return [(f * slabs + s, g * slabs + r) for f, g in freq_pairs for s, r in space_pairs]


def near_sums(keep, give, near_pairs):
    freqs, slabs = lax.axis_size("freq"), lax.axis_size("space")
    own, other = pair_sum(keep, lax.ppermute(give, "freq", [(i, i ^ 1) for i in range(freqs)]))
    across = [(i, i ^ 2) for i in range(freqs)]
    swaps = [p for a, b in near_pairs for p in ((a, b), (b, a))]
    from_own = lax.ppermute(other, "freq", across)
    beyond = lax.ppermute(own, "space", swaps)
    from_beyond = lax.ppermute(other, ("freq", "space"), both(across, swaps, slabs))
    return [own, from_own], [beyond, from_beyond]


def hbm(block):
    return pltpu.with_memory_space_constraint(block, pltpu.HBM)


def split_kernel(side_ref, found_ref, send_ref, keep_ref):
    half = keep_ref.shape[0]
    which = side_ref[1] // 2 % 2
    for ref, side in ((keep_ref, which), (send_ref, 1 - which)):
        for piece in range(half):
            at = side * half + piece
            ref[piece] = found_ref[at] + found_ref[2 * half + at]


def split(sides, found):
    shape = (found.shape[0] // 4,) + found.shape[1:]
    return pl.pallas_call(
        split_kernel,
        in_specs=[pl.BlockSpec(memory_space=pltpu.SMEM), pl.BlockSpec(memory_space=pltpu.VMEM)],
        out_specs=[pl.BlockSpec(memory_space=pltpu.VMEM)] * 2,
        out_shape=[pltpu.VMEM(shape, jnp.float32)] * 2,
        compiler_params=pltpu.CompilerParams(vmem_limit_bytes=SMALL_VMEM),
        cost_estimate=QUICK,
    )(sides, found)


def base_kernel(side_ref, keep_ref, found_ref, *refs):
    base_ref, near_ref, far_ref = refs[-3:]
    slab, depth = base_ref.shape[0], near_ref.shape[0]
    base_ref[...] = keep_ref[0] + found_ref[0]
    start = (1 - side_ref[0]) * (slab - depth)
    near_ref[...] = base_ref[pl.ds(start, depth)]
    far_ref[...] = base_ref[pl.ds(slab - depth - start, depth)]


def finish_base(sides, keep, found, after):
    _, slab, tall, lanes = keep.shape
    return pl.pallas_call(
        base_kernel,
        in_specs=[pl.BlockSpec(memory_space=pltpu.SMEM)]
        + [pl.BlockSpec(memory_space=pltpu.VMEM)] * 2
        + [pl.BlockSpec(memory_space=pl.ANY)] * len(after),
        out_specs=[pl.BlockSpec(memory_space=pltpu.VMEM)] * 3,
        out_shape=[pltpu.VMEM((count, tall, lanes), jnp.float32) for count in (slab, 3, 3)],
        compiler_params=pltpu.CompilerParams(vmem_limit_bytes=SMALL_VMEM),
        cost_estimate=QUICK,
    )(sides, keep, found, *after)


def band_sum(sides, turns):
    count = lax.axis_size("freq")
    groups = [[i, i + 1] for i in range(0, count, 2)]
    send, keep = split(sides, lax.all_to_all(turns, "freq", 0, 0, axis_index_groups=groups, tiled=True))
    found = lax.ppermute(send, "freq", [(i, i ^ 2) for i in range(count)])
    return *finish_base(sides, keep, found, []), keep


def local(saved_modes, mode_gains):
    _, modes, kinds, halves, parts, slab, rows, lanes = saved_modes.shape
    freqs = lax.axis_size("freq")
    slabs = lax.axis_size("space")
    factor = -2.0 / (saved_modes.shape[0] * freqs * modes)
    weights = (factor / 8.0) * mode_gains
    place = lax.axis_index("space")
    odd = place % 2
    near_pairs = [(i, i + 1) for i in range(0, slabs - 1, 2)]
    far_pairs = [(i, i + 1) for i in range(1, slabs - 1, 2)]

    def outer(plane, begin, count):
        start = (0, begin, 0, 0, 0, plane, 0, 0)
        found = lax.dynamic_slice(saved_modes, start, (1, count, kinds, halves, parts, 1, rows, lanes))
        return found.reshape((count, kinds, halves, parts, rows, lanes))

    near_plane = jnp.where(odd == 0, slab - 1, 0)
    half = modes // 4 or 1
    groups = [(0, half), (half, modes - half)]
    (first_out,) = planes(saved_modes, near_plane, [(0, 1)], [])
    (near_out,) = planes(saved_modes, near_plane, [(1, modes - 1)], [first_out])
    near_halos = [swap(block, "space", near_pairs) for block in (first_out, near_out)]
    far_outs = planes(saved_modes, slab - 1 - near_plane, groups, [near_out])
    far_halos = [swap(block, "space", far_pairs) for block in far_outs]

    sides = jnp.stack([odd, lax.axis_index("freq")]).astype(jnp.int32)
    sens, _, near_edges, far_edges = interior(saved_modes, weights, sides, 0, modes, [], far_outs)
    turns = finish_far(sides, weights, groups, far_edges, far_halos, sens, freqs)
    base, near, far, keep = band_sum(sides, turns)
    near, far = swap(near, "space", near_pairs), swap(far, "space", far_pairs)
    where = jnp.stack([odd, place * slab, lax.axis_index("freq") * (rows // freqs)]).astype(jnp.int32)
    smoothed = smooth(where, base, near, far, slab * slabs, rows)

    keep, give = finish_near(sides, weights, *fetch([near_edges], [keep]), near_halos, freqs)
    return add_near(where, *near_sums(keep, give, near_pairs), smoothed, rows)


def solution(mesh):
    in_specs = (P("freq", None, None, None, None, "space", None, None), P("freq", None))
    out_specs = P("space", "freq", None)
    return jax.shard_map(local, mesh=mesh, in_specs=in_specs, out_specs=out_specs, check_vma=False)
```
